512 devices in a mesh: dp: 8 (over y_lo, core), tm: 64 (over x, y_hi, z).
Axes of the slice: x: 4, y: 8 (y_hi: 2, y_lo: 4; y = y_hi * 4 + y_lo), z: 8, core: 2. Of those that a mesh axis runs over, the one named last changes fastest.
Arguments:
- queries: bfloat16 [8, 64, 128, 576], P('dp', 'tm'), may hold values from -48 to 48
- keys: bfloat16 [8, 64, 128, 576], P('dp', 'tm'), may hold values from -48 to 48
- values: bfloat16 [8, 64, 128, 576], P('dp', 'tm'), may hold values from -6 to 6
- out_weight: bfloat16 [576, 1152], P('tm', 'dp'), may hold values from -0.25 to 0.25
- upstream: bfloat16 [8, 64, 128, 1152], P('dp', 'tm'), may hold values from -16 to 16
- timestep: int32 [8], P('dp'), may hold values from 0 to 999
Outputs:
- output: bfloat16 [8, 64, 128, 1152], P('dp', 'tm')
- query_grad: bfloat16 [8, 64, 128, 576], P('dp', 'tm')
- key_grad: bfloat16 [8, 64, 128, 576], P('dp', 'tm')
- value_grad: bfloat16 [8, 64, 128, 576], P('dp', 'tm')
- weight_grad: float32 [576, 1152], P('tm', 'dp')
The draws below stay inside these ranges and needn't reach their ends.
All inputs are finite; a program needn't handle non-finite values.
Results may differ from the reference program's by a relative error of at most 0.0065.
Values may be sent and summed in bfloat16 or wider, within the bound.
No kernel may reach another device: no remote copies, remote signals or barrier semaphores. Data moves between devices by JAX's collectives and lax.ppermute only.
A program may use at most 64 MiB of HBM per device.

```python
import jax
import jax.numpy as jnp
from jax import lax

D = 1152
HEADS = 8
HEAD = 72
HD = 576
PATCHES = 128
FRAMES = 64
CLIPS = 8


def draw_keys(key, part):
    key = jax.random.fold_in(key, 11)
    own = jnp.clip(jax.random.normal(key, (CLIPS, FRAMES, PATCHES, HD), jnp.float32), -6.0, 6.0)
    return own.astype(jnp.bfloat16)


def draw_queries(key, part):
    key = jax.random.fold_in(key, 7)
    own = jnp.clip(jax.random.normal(key, (CLIPS, FRAMES, PATCHES, HD), jnp.float32), -6.0, 6.0)
    return own.astype(jnp.bfloat16)


def with_ends(array, stream_key, low, top_value):
    spot = [jax.random.randint(jax.random.fold_in(stream_key, axis), (), 0, length) for axis, length in enumerate(array.shape)]
    longest = array.shape.index(max(array.shape))
    beside = spot[:longest] + [(spot[longest] + 1) % array.shape[longest]] + spot[longest + 1:]
    return array.at[tuple(spot)].set(low).at[tuple(beside)].set(top_value)


def with_spikes(values, stream_key, source, target, shards_of, factor):
    def block_of(dim):
        return (jnp.arange(values.shape[dim]) // (values.shape[dim] // shards_of)).reshape((-1,) + (1,) * (values.ndim - 1 - dim))

    one_side = jax.random.permutation(stream_key, shards_of)[block_of(target)]
    second = (block_of(target) + shards_of // 2) % shards_of
    return jnp.where((block_of(source) == one_side) | (block_of(source) == second), factor * values, values)


def levels(stream_key, shape, shards, low, high):
    loudness, own = 1.0, jax.random.fold_in(stream_key, 6)
    for axis_at, shards_of in shards:
        heights = jnp.exp(jax.random.uniform(jax.random.fold_in(own, axis_at), (shards_of,), jnp.float32, low / len(shards), high / len(shards)))
        loudness = loudness * jnp.repeat(heights, shape[axis_at] // shards_of).reshape([-1 if axis == axis_at else 1 for axis in range(len(shape))])
    return loudness


def gaussian(own_key, shape, width, limit, pieces=(), dtype=jnp.bfloat16):
    entries = width * jax.random.normal(own_key, shape, jnp.float32)
    if pieces:
        entries = entries * levels(own_key, shape, pieces, -0.22, 0.18)
    return jnp.clip(entries, -limit, limit).astype(dtype)


def bell_draw_with(stream_key, extent, width, limit, cuts, heavy, dtype=jnp.bfloat16):
    entries = width * jax.random.normal(stream_key, extent, jnp.float32)
    if cuts:
        entries = entries * levels(stream_key, extent, cuts, -0.22, 0.18)
    return jnp.clip(with_spikes(entries, jax.random.fold_in(stream_key, 3), *heavy), -limit, limit).astype(dtype)


def setup_inputs(seed: int = 0) -> dict:
    key_of = jax.random.split(jax.random.key(seed), 7)
    return {
        "queries": draw_queries(jax.random.fold_in(key_of[6], 71), 0),
        "keys": draw_keys(jax.random.fold_in(key_of[6], 71), 0),
        "values": gaussian(key_of[2], (CLIPS, FRAMES, PATCHES, HD), 1.0, 6.0, ((0, 8), (1, 64))),
        "out_weight": gaussian(key_of[3], (HD, D), HD ** -0.5, 0.25, ((0, 64), (1, 8))),
        "upstream": bell_draw_with(key_of[4], (CLIPS, FRAMES, PATCHES, D), 1.0, 16.0, ((0, 8), (1, 64)), (1, 3, 64, 4.0)),
        "timestep": with_ends(jax.random.randint(key_of[5], (CLIPS,), 0, 1000), jax.random.fold_in(key_of[5], 1), 0, 999).astype(jnp.int32),
    }


def gate_table(timestep):
    freq = jnp.exp(-jnp.log(10000.0) * jnp.arange(D).astype(jnp.float32) / D)
    return 1.5 + jnp.sin(timestep.astype(jnp.float32)[:, None] * freq[None, :])

def clip_pass(operands):
    query, key_part, value, grad_in = operands
    frames = query.shape[0]
    qh = query.reshape(frames, PATCHES, HEADS, HEAD).astype(jnp.float32)
    kh = key_part.reshape(frames, PATCHES, HEADS, HEAD).astype(jnp.float32)
    vh = value.reshape(frames, PATCHES, HEADS, HEAD).astype(jnp.float32)
    factor = 1.0 / jnp.sqrt(jnp.float32(HEAD))
    scores = jnp.einsum('fphe,gphe->phfg', qh, kh) * factor
    shifted = scores - lax.optimization_barrier(jnp.max(scores, axis=-1, keepdims=True))
    expd = jnp.exp(shifted)
    probs = expd / lax.optimization_barrier(jnp.sum(expd, axis=-1, keepdims=True))
    probs_low = probs.astype(jnp.bfloat16).astype(jnp.float32)
    attended = jnp.einsum('phfg,gphe->fphe', probs_low, vh).astype(jnp.bfloat16)
    return (attended.reshape(frames, PATCHES, HEADS * HEAD), probs, probs_low, qh, kh, vh)

def clip_back(operands):
    query, key_part, value, grad_att = operands
    frames = query.shape[0]
    attended, probs, probs_low, qh, kh, vh = clip_pass((query, key_part, value, grad_att))
    gh = grad_att.reshape(frames, PATCHES, HEADS, HEAD).astype(jnp.float32)
    factor = 1.0 / jnp.sqrt(jnp.float32(HEAD))
    prob_grad = jnp.einsum('fphe,gphe->phfg', gh, vh)
    value_grad = jnp.einsum('phfg,fphe->gphe', probs_low, gh).astype(jnp.bfloat16)
    inner = lax.optimization_barrier(jnp.sum(probs * prob_grad, axis=-1, keepdims=True))
    score_grad = (probs * (prob_grad - inner)).astype(jnp.bfloat16).astype(jnp.float32)
    query_grad = (jnp.einsum('phfg,gphe->fphe', score_grad, kh) * factor).astype(jnp.bfloat16)
    key_grad = (jnp.einsum('phfg,fphe->gphe', score_grad, qh) * factor).astype(jnp.bfloat16)
    shape = (frames, PATCHES, HEADS * HEAD)
    return (query_grad.reshape(shape), key_grad.reshape(shape), value_grad.reshape(shape))

def reference(queries, keys, values, out_weight, upstream, timestep):
    attended = lax.map(lambda ops: clip_pass(ops)[0], (queries, keys, values, queries))
    gate = gate_table(timestep)
    clips = queries.shape[0]
    flat_att = attended.reshape(clips, -1, HEADS * HEAD)
    proj = jnp.einsum('cth,hd->ctd', flat_att.astype(jnp.float32), out_weight.astype(jnp.float32))
    output = (gate[:, None, :] * proj).astype(jnp.bfloat16).reshape(upstream.shape)
    scaled = (gate[:, None, :] * upstream.reshape(clips, -1, D).astype(jnp.float32)).astype(jnp.bfloat16)
    attended_grad = jnp.einsum('ctd,hd->cth', scaled.astype(jnp.float32), out_weight.astype(jnp.float32)).astype(jnp.bfloat16)
    weight_grad = jnp.dot(flat_att.reshape(-1, HEADS * HEAD).T, scaled.reshape(-1, D), preferred_element_type=jnp.float32)
    attended_grad = attended_grad.reshape(queries.shape)
    query_grad, key_grad, value_grad = lax.map(clip_back, (queries, keys, values, attended_grad))
    return (output, query_grad, key_grad, value_grad, weight_grad)
```

```python
import jax
import jax.numpy as jnp
from jax import lax
from jax.sharding import PartitionSpec as P

D = 1152
HEADS = 8
CORES = 2
F32 = jnp.float32
BF16 = jnp.bfloat16


def slab_scores(query_slab, key_slab):
    frames, patches, feats = query_slab.shape
    qh = query_slab.reshape(frames, patches, HEADS, feats // HEADS)
    kh = key_slab.reshape(frames, patches, HEADS, feats // HEADS)
    factor = 1.0 / jnp.sqrt(F32(feats // HEADS))
    scores = jnp.einsum("fphe,gphe->phfg", qh, kh, preferred_element_type=F32) * factor
    shifted = scores - jnp.max(scores, axis=-1, keepdims=True)
    expd = jnp.exp(shifted)
    return expd / jnp.sum(expd, axis=-1, keepdims=True)


def gate_table(timestep):
    freq = jnp.exp(-jnp.log(10000.0) * jnp.arange(D).astype(F32) / D)
    return 1.5 + jnp.sin(timestep.astype(F32)[:, None] * freq[None, :])


def shards(dp_size, tm_size, queries, keys, values, out_weight, upstream, timestep):
    patches, feats = queries.shape[2:]
    head_size = feats // HEADS
    per = patches // tm_size
    factor = 1.0 / jnp.sqrt(F32(head_size))
    lines = dp_size // CORES
    dp = lax.axis_index("dp")
    line, core = dp // CORES, dp % CORES

    def shift_line(x, s):
        return lax.ppermute(x, "dp", [(d, (d + CORES * s) % dp_size) for d in range(dp_size)])

    def swap_core(x):
        return lax.ppermute(x, "dp", [(d, d ^ 1) for d in range(dp_size)])

    rows, cols = out_weight.shape
    half = lines * cols
    got = [out_weight] + [shift_line(out_weight, s) for s in range(1, lines)]
    around = jnp.stack([got[-i % lines] for i in range(2 * lines - 1)], axis=1)
    own_rows = lax.dynamic_slice_in_dim(around, (lines - line) % lines, lines, axis=1)
    own_rows = jnp.broadcast_to(
        own_rows.reshape(1, per, rows * half // per), (tm_size, per, rows * half // per)
    )
    sent = jnp.concatenate(
        [x.reshape(tm_size, per, x.shape[-1]) for x in (queries, keys, values, upstream)] + [own_rows],
        axis=2,
    )
    slab = lax.all_to_all(sent, "tm", split_axis=0, concat_axis=0, tiled=True)
    query_slab = slab[:, :, :feats]
    key_slab = slab[:, :, feats : 2 * feats]
    value_slab = slab[:, :, 2 * feats : 3 * feats]
    up_slab = slab[:, :, 3 * feats : 3 * feats + D]
    own_half = slab[:, :, 3 * feats + D :].reshape(tm_size * rows, half)
    other_half = swap_core(own_half)
    even = jnp.where(core == 0, own_half, other_half).reshape(feats, lines, 1, cols)
    odd = jnp.where(core == 0, other_half, own_half).reshape(feats, lines, 1, cols)
    weight = jnp.concatenate([even, odd], axis=2).reshape(feats, D)

    split_shape = (tm_size, per, HEADS, head_size)
    vh = value_slab.reshape(split_shape)
    probs = slab_scores(query_slab, key_slab)
    probs_low = probs.astype(BF16)
    attended = jnp.einsum("phfg,gphe->fphe", probs_low, vh, preferred_element_type=F32)
    attended = attended.astype(BF16).reshape(tm_size * per, feats)
    gate = gate_table(timestep)
    scaled = (gate * up_slab.reshape(tm_size * per, D)).astype(BF16)
    by_core = scaled.reshape(-1, lines, CORES, cols)
    mine = jnp.where(core == 0, by_core[:, :, 0], by_core[:, :, 1]).reshape(-1, half)
    theirs = jnp.where(core == 0, by_core[:, :, 1], by_core[:, :, 0]).reshape(-1, half)
    swapped = swap_core(jnp.concatenate([attended, theirs], axis=1))
    att_rows = jnp.concatenate([attended, swapped[:, :feats]], axis=0)
    scaled_rows = jnp.concatenate([mine, swapped[:, feats:]], axis=0)
    share = lax.dot_general(
        att_rows, scaled_rows, (((0,), (0,)), ((), ())), preferred_element_type=F32
    )
    share = share.astype(BF16).reshape(tm_size, per, rows * half // per)

    attended_grad = lax.dot_general(
        scaled, weight, (((1,), (1,)), ((), ())), preferred_element_type=F32
    ).astype(BF16)
    gh = attended_grad.reshape(split_shape)
    prob_grad = jnp.einsum("fphe,gphe->phfg", gh, vh, preferred_element_type=F32)
    value_grad = jnp.einsum("phfg,fphe->gphe", probs_low, gh, preferred_element_type=F32)
    inner = jnp.sum(probs * prob_grad, axis=-1, keepdims=True)
    score_grad = (probs * (prob_grad - inner)).astype(BF16)
    qh = query_slab.reshape(split_shape)
    kh = key_slab.reshape(split_shape)
    query_grad = jnp.einsum("phfg,gphe->fphe", score_grad, kh, preferred_element_type=F32) * factor
    key_grad = jnp.einsum("phfg,fphe->gphe", score_grad, qh, preferred_element_type=F32) * factor
    back = jnp.concatenate(
        [
            x.astype(BF16).reshape(tm_size, per, feats)
            for x in (attended, query_grad, key_grad, value_grad)
        ]
        + [share],
        axis=2,
    )
    frame = lax.all_to_all(back, "tm", split_axis=0, concat_axis=0, tiled=True)
    att_frame, query_back, key_back, value_back = (
        frame[:, :, i * feats : (i + 1) * feats].reshape(patches, feats) for i in range(4)
    )
    proj = lax.dot_general(att_frame, weight, (((1,), (0,)), ((), ())), preferred_element_type=F32)
    output = (gate * proj).astype(BF16).reshape(upstream.shape)
    total = jnp.sum(frame[:, :, 4 * feats :].astype(F32), axis=0).reshape(rows, lines, cols)
    weight_grad = lax.dynamic_index_in_dim(total, line, 1, keepdims=False)
    for s in range(1, lines):
        piece = lax.dynamic_index_in_dim(total, (line + s) % lines, 1, keepdims=False)
        weight_grad = weight_grad + shift_line(piece, s)
    shape = queries.shape
    return (
        output,
        query_back.reshape(shape),
        key_back.reshape(shape),
        value_back.reshape(shape),
        weight_grad,
    )


def solution(mesh):
    sizes = mesh.shape["dp"], mesh.shape["tm"]

    def body(*args):
        return shards(*sizes, *args)

    act = P("dp", "tm", None, None)
    return jax.shard_map(
        body,
        mesh=mesh,
        in_specs=(act, act, act, P("tm", "dp"), act, P("dp")),
        out_specs=(act, act, act, act, P("tm", "dp")),
        check_vma=False,
    )
```

```python
import functools

import jax
import jax.numpy as jnp
import numpy as np
from jax import lax
from jax.experimental import pallas as pl
from jax.experimental.pallas import tpu as pltpu
from jax.sharding import PartitionSpec as P

D = 1152
HEADS = 8
HEAD = 72
HD = HEADS * HEAD
CORES = 2
LINES = 4
SOURCES = 64
PAIR = 2
TOKENS = SOURCES * PAIR
ROWS = HD // SOURCES
COLS = D // (CORES * LINES)
HALF = D // CORES
SPLIT = (ROWS + 1) // 2
F32 = jnp.float32
BF16 = jnp.bfloat16

W_LANES = 768
AT_U = W_LANES
AT_Q = AT_U + D
AT_K = AT_Q + HD
AT_V = AT_K + HD
IN_LANES = AT_V + HD
AT_G = 4 * HD
OUT_LANES = AT_G + SPLIT * COLS


def iota(shape, dim):
    return lax.broadcasted_iota(jnp.int32, shape, dim)


def order_matrix():
    feature, place = iota((HD, HD), 0), iota((HD, HD), 1)
    return (feature == ROWS * (place & (SOURCES - 1)) + (place >> 6)).astype(BF16)


def head_mask(head):
    return (((iota((1, HD), 1) & (SOURCES - 1)) >> 3) == head).astype(BF16)


def dot(a, b, dims, kind=F32):
    return lax.dot_general(a, b, (dims, ((), ())), preferred_element_type=F32).astype(kind)


NN = ((1,), (0,))
NT = ((1,), (1,))
TN = ((0,), (0,))


def spread(x):
    return x.reshape(SOURCES, PAIR, x.shape[-1])


def pack_kernel(
    core_ref, line_ref, w0, w1, w2, w3, q_ref, k_ref, v_ref, u_ref, x_ref, lines, feats, up, sems
):
    copies = []
    for n, ref in enumerate((q_ref, k_ref, v_ref)):
        for h in range(2):
            part = pl.ds(h * (HD // 2), HD // 2)
            copies.append(
                pltpu.make_async_copy(ref.at[part], feats.at[n, part], sems.at[2 * n + h])
            )
    for h in range(4):
        part = pl.ds(h * (TOKENS // 4), TOKENS // 4)
        copies.append(pltpu.make_async_copy(u_ref.at[part], up.at[part], sems.at[6 + h]))
    for copy in copies:
        copy.start()
    for s, ref in enumerate((w0, w1, w2, w3)):
        w = ref[...].astype(F32)
        rows = [w[i : i + 1] for i in range(ROWS)]
        for j in range(PAIR):
            part = rows[SPLIT * j : SPLIT * (j + 1)]
            pad = jnp.zeros((1, W_LANES - len(part) * COLS), F32)
            lines[s, j : j + 1, :] = jnp.concatenate(part + [pad], axis=1)
    count = TOKENS // LINES
    odd = (iota((count, W_LANES), 0) & 1) == 1
    line, parts = line_ref[0], []
    for b in range(LINES):
        pair = lines[lax.rem(line - b + LINES, LINES)]
        parts.append(jnp.where(odd, pair[1:2], pair[0:1]))
    x_ref[:, :, :W_LANES] = spread(jnp.concatenate(parts, axis=0).astype(BF16))

    order = order_matrix()
    for n, at in enumerate((AT_Q, AT_K, AT_V)):
        copies[2 * n].wait()
        copies[2 * n + 1].wait()
        x_ref[:, :, at : at + HD] = spread(dot(feats[n], order, TN, BF16))
    for copy in copies[6:]:
        copy.wait()
    first = core_ref[0] == 0
    mine, theirs = [], []
    for line in range(LINES):
        a = up[:, (2 * line) * COLS : (2 * line + 1) * COLS]
        b = up[:, (2 * line + 1) * COLS : (2 * line + 2) * COLS]
        mine.append(jnp.where(first, a, b))
        theirs.append(jnp.where(first, b, a))
    x_ref[:, :, AT_U : AT_U + D] = spread(jnp.concatenate(mine + theirs, axis=1))


def weight_kernel(x_ref, own_ref, r1_ref, r2_ref, r3_ref, w_ref, raw):
    for s, ref in enumerate((own_ref, r1_ref, r2_ref, r3_ref)):
        raw[s] = ref[...].reshape(TOKENS, W_LANES)
    x = x_ref[0]
    pick = iota((SOURCES, TOKENS), 1) - PAIR * iota((SOURCES, TOKENS), 0)
    for b in range(LINES):
        block = raw[lax.rem(x - b + LINES, LINES)]
        for j in range(PAIR):
            part = dot((pick == j).astype(BF16), block, NN, BF16)
            for i in range(SPLIT * j, min(SPLIT * (j + 1), ROWS)):
                lane = (i - SPLIT * j) * COLS
                w_ref[i * SOURCES : (i + 1) * SOURCES, b * COLS : (b + 1) * COLS] = part[
                    :, lane : lane + COLS
                ]


def rows_of(x_ref, at, lanes):
    return x_ref[:, :, at : at + lanes].reshape(TOKENS, lanes)


def scale_upstream(x_ref, gate_ref):
    return (gate_ref[...] * rows_of(x_ref, AT_U, D).astype(F32)).astype(BF16)


def forward_kernel(gate_ref, x_ref, probs_ref, swap_ref, mine_ref):
    q, k, v = (rows_of(x_ref, at, HD) for at in (AT_Q, AT_K, AT_V))
    factor = 1.0 / jnp.sqrt(F32(HEAD))
    same = ((iota((TOKENS, TOKENS), 0) ^ iota((TOKENS, TOKENS), 1)) & 1) == 0
    low, v_rows = [], []
    for h in range(HEADS):
        mask = head_mask(h)
        scores = dot(q * mask, k, NT) * factor
        scores = jnp.where(same, scores, -jnp.inf)
        expd = jnp.exp(scores - jnp.max(scores, axis=-1, keepdims=True))
        probs = expd / jnp.sum(expd, axis=-1, keepdims=True)
        probs_ref[h] = probs
        low.append(probs.astype(BF16))
        v_rows.append(v * mask)
    attended = dot(jnp.concatenate(low, axis=1), jnp.concatenate(v_rows, axis=0), NN, BF16)
    scaled = scale_upstream(x_ref, gate_ref)
    swap_ref[:, :HD] = attended
    swap_ref[:, HD:] = scaled[:, HALF:]
    mine_ref[...] = scaled[:, :HALF]


def share_kernel(line_ref, swap_ref, got_ref, mine_ref, o0_ref, o1_ref, o2_ref, o3_ref, packed):
    share = dot(swap_ref[:, :HD], mine_ref[...], TN) + dot(got_ref[:, :HD], got_ref[:, HD:], TN)
    share = share.astype(BF16)
    for b in range(LINES):
        for i in range(ROWS):
            packed[b, :, i * COLS : (i + 1) * COLS] = share[
                i * SOURCES : (i + 1) * SOURCES, b * COLS : (b + 1) * COLS
            ]
    line = line_ref[0]
    for s, ref in enumerate((o0_ref, o1_ref, o2_ref, o3_ref)):
        ref[...] = packed[lax.rem(line + s, LINES)]


def backward_kernel(gate_ref, x_ref, probs_ref, wm_ref, wt_ref, dq_ref, dk_ref, dv_ref):
    q, k, v = (rows_of(x_ref, at, HD) for at in (AT_Q, AT_K, AT_V))
    factor = 1.0 / jnp.sqrt(F32(HEAD))
    scaled = scale_upstream(x_ref, gate_ref)
    grad = dot(scaled[:, :HALF], wm_ref[...], NT) + dot(scaled[:, HALF:], wt_ref[...], NT)
    grad = grad.astype(BF16)
    low, score_grads, g_rows, q_rows, k_rows = [], [], [], [], []
    for h in range(HEADS):
        mask = head_mask(h)
        g_head = grad * mask
        probs = probs_ref[h]
        prob_grad = dot(g_head, v, NT)
        inner = jnp.sum(probs * prob_grad, axis=-1, keepdims=True)
        score_grads.append((probs * (prob_grad - inner)).astype(BF16))
        low.append(probs.astype(BF16))
        g_rows.append(g_head)
        q_rows.append(q * mask)
        k_rows.append(k * mask)
    wide = jnp.concatenate(score_grads, axis=1)
    tall = jnp.concatenate(score_grads, axis=0)
    dq_ref[...] = (dot(wide, jnp.concatenate(k_rows, axis=0), NN) * factor).astype(BF16)
    dk_ref[...] = (dot(tall, jnp.concatenate(q_rows, axis=0), TN) * factor).astype(BF16)
    dv_ref[...] = dot(jnp.concatenate(low, axis=0), jnp.concatenate(g_rows, axis=0), TN, BF16)


def sum_kernel(p0_ref, p1_ref, p2_ref, p3_ref, o_ref):
    total = sum(ref[...].astype(F32) for ref in (p0_ref, p1_ref, p2_ref, p3_ref)).astype(BF16)
    lanes = SPLIT * COLS
    pad = jnp.zeros((SOURCES, PAIR * lanes - ROWS * COLS), BF16)
    low = jnp.concatenate([total[:, lanes:], pad], axis=1)
    put = iota((TOKENS, SOURCES), 0) - PAIR * iota((TOKENS, SOURCES), 1)
    mixed = dot((put == 0).astype(BF16), total[:, :lanes], NN) + dot((put == 1).astype(BF16), low, NN)
    o_ref[...] = mixed.astype(BF16)


def back_kernel(swap_ref, dq_ref, dk_ref, dv_ref, sum_ref, x_ref):
    x_ref[:, :, :HD] = spread(swap_ref[:, :HD])
    for n, ref in enumerate((dq_ref, dk_ref, dv_ref)):
        x_ref[:, :, (n + 1) * HD : (n + 2) * HD] = spread(ref[...])
    x_ref[:, :, AT_G:OUT_LANES] = spread(sum_ref[...])


def final_kernel(
    core_ref, gate_ref, z_ref, wm_ref, wt_ref, out_ref, dq_ref, dk_ref, dv_ref, wg_ref
):
    att = rows_of(z_ref, 0, HD)
    gate = gate_ref[...]
    mine = (gate[:, :HALF] * dot(att, wm_ref[...], NN)).astype(BF16)
    theirs = (gate[:, HALF:] * dot(att, wt_ref[...], NN)).astype(BF16)
    first = core_ref[0] == 0
    parts = []
    for line in range(LINES):
        a = mine[:, line * COLS : (line + 1) * COLS]
        b = theirs[:, line * COLS : (line + 1) * COLS]
        parts += [jnp.where(first, a, b), jnp.where(first, b, a)]
    out_ref[...] = jnp.concatenate(parts, axis=1)
    order = order_matrix()
    for n, ref in enumerate((dq_ref, dk_ref, dv_ref)):
        ref[...] = dot(order, rows_of(z_ref, (n + 1) * HD, HD), NT, BF16)
    pick = ((iota((8, TOKENS), 1) & 1) == iota((8, TOKENS), 0)).astype(BF16)
    sums = dot(pick, rows_of(z_ref, AT_G, SPLIT * COLS), NN)
    for i in range(ROWS):
        j, lane = i // SPLIT, (i % SPLIT) * COLS
        wg_ref[i : i + 1, :] = sums[j : j + 1, lane : lane + COLS]


def call(kernel, outs, args, scalars=0, far=0, scratch=(), flops=10**8, limit=24):
    smem = [pl.BlockSpec(memory_space=pltpu.SMEM)] * scalars
    vmem = [pl.BlockSpec(memory_space=pltpu.VMEM)] * (len(args) - scalars - far)
    hbm = [pl.BlockSpec(memory_space=pltpu.HBM)] * far
    moved = sum(int(np.prod(x.shape)) * x.dtype.itemsize for x in [*args, *outs])
    single = len(outs) == 1
    out_spec = [pl.BlockSpec(memory_space=pltpu.VMEM)] * len(outs)
    return pl.pallas_call(
        kernel,
        out_shape=outs[0] if single else outs,
        in_specs=smem + vmem + hbm,
        out_specs=out_spec[0] if single else out_spec,
        scratch_shapes=scratch,
        cost_estimate=pl.CostEstimate(flops=flops, bytes_accessed=moved, transcendentals=0),
        compiler_params=pltpu.CompilerParams(vmem_limit_bytes=limit * 1024 * 1024),
    )(*args)


def shape(*dims, kind=BF16):
    return jax.ShapeDtypeStruct(dims, kind)


def column_order():
    cols = np.arange(D).reshape(LINES, CORES, COLS)
    return [np.concatenate([cols[:, c].ravel(), cols[:, 1 - c].ravel()]) for c in range(CORES)]


def shards(dp_size, queries, keys, values, out_weight, upstream, timestep):
    dp = lax.axis_index("dp")
    line, core = (dp // CORES).astype(jnp.int32), (dp % CORES).astype(jnp.int32)
    line_s, core_s = line.reshape(1), core.reshape(1)
    x_s = (lax.axis_index("tm") // (SOURCES // LINES)).astype(jnp.int32).reshape(1)

    def shift_line(x, s):
        return lax.ppermute(x, "dp", [(d, (d + CORES * s) % dp_size) for d in range(dp_size)])

    def shift_x(x, s):
        step = SOURCES // LINES
        return lax.ppermute(x, "tm", [(t, (t + step * s) % SOURCES) for t in range(SOURCES)])

    def swap_core(x):
        return lax.ppermute(x, "dp", [(d, d ^ 1) for d in range(dp_size)])

    orders = [o.astype(np.float32) for o in column_order()]
    index = jnp.where(core == 0, orders[0], orders[1])
    freq = jnp.exp(-jnp.log(10000.0) * index / D)
    gate = (1.5 + jnp.sin(timestep.astype(F32)[0] * freq)).reshape(1, D)

    flat = [x.reshape(TOKENS, HD).T for x in (queries, keys, values)]
    weights = [out_weight] + [shift_line(out_weight, s) for s in range(1, LINES)]
    sent = call(
        pack_kernel,
        [shape(SOURCES, PAIR, IN_LANES)],
        (core_s, line_s, *weights, *flat, upstream.reshape(TOKENS, D)),
        scalars=2,
        far=4,
        limit=60,
        scratch=[
            pltpu.VMEM((LINES, 8, W_LANES), F32),
            pltpu.VMEM((3, HD, TOKENS), BF16),
            pltpu.VMEM((TOKENS, D), BF16),
            pltpu.SemaphoreType.DMA((10,)),
        ],
    )
    slab = lax.all_to_all(sent, "tm", split_axis=0, concat_axis=0, tiled=True)

    probs, swap, mine = call(
        forward_kernel,
        [shape(HEADS, TOKENS, TOKENS, kind=F32), shape(TOKENS, HD + HALF), shape(TOKENS, HALF)],
        (gate, slab),
    )
    got = swap_core(swap)
    own_raw, _ = lax.optimization_barrier((slab[:, :, :W_LANES], swap))
    raws = [own_raw] + [shift_x(own_raw, s) for s in range(1, LINES)]
    pieces = call(
        share_kernel,
        [shape(SOURCES, ROWS * COLS)] * LINES,
        (line_s, swap, got, mine),
        scalars=1,
        scratch=[pltpu.VMEM((LINES, SOURCES, ROWS * COLS), BF16)],
    )
    sums = [pieces[0]] + [shift_line(pieces[s], s) for s in range(1, LINES)]
    x_late, _ = lax.optimization_barrier((x_s, pieces[0]))
    w_mine = call(
        weight_kernel,
        [shape(HD, HALF)],
        (x_late, *raws),
        scalars=1,
        scratch=[pltpu.VMEM((LINES, TOKENS, W_LANES), BF16)],
    )
    w_theirs = swap_core(w_mine)
    grads = call(
        backward_kernel, [shape(TOKENS, HD)] * 3, (gate, slab, probs, w_mine, w_theirs), flops=10**9
    )
    total = call(sum_kernel, [shape(TOKENS, SPLIT * COLS)], sums, flops=10**10)
    back = call(back_kernel, [shape(SOURCES, PAIR, OUT_LANES)], (swap, *grads, total))
    frame = lax.all_to_all(back, "tm", split_axis=0, concat_axis=0, tiled=True)
    output, dq, dk, dv, weight_grad = call(
        final_kernel,
        [shape(TOKENS, D)] + [shape(HD, TOKENS)] * 3 + [shape(ROWS, COLS, kind=F32)],
        (core_s, gate, frame, w_mine, w_theirs),
        scalars=1,
    )
    dims = queries.shape
    return (output.reshape(upstream.shape), *(x.T.reshape(dims) for x in (dq, dk, dv)), weight_grad)


def solution(mesh):
    act = P("dp", "tm", None, None)
    return jax.shard_map(
        functools.partial(shards, mesh.shape["dp"]),
        mesh=mesh,
        in_specs=(act, act, act, P("tm", "dp"), act, P("dp")),
        out_specs=(act, act, act, act, P("tm", "dp")),
        check_vma=False,
    )
```

```python
import jax
import jax.numpy as jnp
import numpy as np
from jax import lax
from jax.experimental import pallas as pl
from jax.experimental.pallas import tpu as pltpu
from jax.sharding import PartitionSpec as P

D = 1152
HEADS = 8
HEAD = 72
HD = HEADS * HEAD
CORES = 2
LINES = 4
SOURCES = 64
PAIR = 2
TOKENS = SOURCES * PAIR
ROWS = HD // SOURCES
COLS = D // (CORES * LINES)
HALF = D // CORES
SPLIT = (ROWS + 1) // 2
F32 = jnp.float32
BF16 = jnp.bfloat16

AXES = {"line": LINES, "core": CORES, "x": 4, "y": 2, "z": 8}
OTHERS = ("x", "y", "z")
W_PEERS = LINES * SOURCES
W_LANES = (ROWS + 1) // 2 * COLS

AT_U = 0
AT_Q = AT_U + D
AT_K = AT_Q + HD
AT_V = AT_K + HD
IN_LANES = AT_V + HD
AT_G = 4 * HD
OUT_LANES = AT_G + SPLIT * COLS


def iota(shape, dim):
    return lax.broadcasted_iota(jnp.int32, shape, dim)


def order_matrix():
    feature, place = iota((HD, HD), 0), iota((HD, HD), 1)
    return (feature == ROWS * (place & (SOURCES - 1)) + (place >> 6)).astype(BF16)


def head_mask(head):
    return (((iota((1, HD), 1) & (SOURCES - 1)) >> 3) == head).astype(BF16)


def dot(a, b, dims, kind=F32):
    return lax.dot_general(a, b, (dims, ((), ())), preferred_element_type=F32).astype(kind)


NN = ((1,), (0,))
NT = ((1,), (1,))
TN = ((0,), (0,))


def spread(x):
    return x.reshape(SOURCES, PAIR, x.shape[-1])


def repeat_kernel(w_ref, x_ref):
    w = w_ref[...].astype(F32)
    rows = [w[i : i + 1] for i in range(ROWS)]
    pair = []
    for j in range(PAIR):
        part = rows[SPLIT * j : SPLIT * (j + 1)]
        part = part + [jnp.zeros((1, COLS), F32)] * (SPLIT - len(part))
        pair.append(jnp.concatenate(part, axis=1))
    odd = (iota((TOKENS, W_LANES), 0) & 1) == 1
    both = spread(jnp.where(odd, pair[1], pair[0]).astype(BF16))
    for b in range(LINES):
        x_ref[b * SOURCES : (b + 1) * SOURCES] = both


def pack_kernel(core_ref, q_ref, k_ref, v_ref, u_ref, x_ref, feats, up, packed, sems):
    copies = []
    for h in range(4):
        part = pl.ds(h * (TOKENS // 4), TOKENS // 4)
        copies.append(pltpu.make_async_copy(u_ref.at[part], up.at[part], sems.at[h]))
    for n, ref in enumerate((q_ref, k_ref, v_ref)):
        for h in range(2):
            part = pl.ds(h * (HD // 2), HD // 2)
            copies.append(
                pltpu.make_async_copy(ref.at[part], feats.at[n, part], sems.at[4 + 2 * n + h])
            )
    for copy in copies:
        copy.start()

    def out(n, at, lanes):
        part = pl.ds(at, lanes)
        return pltpu.make_async_copy(
            packed.at[:, :, part], x_ref.at[:, :, part], sems.at[10 + n]
        )

    outs = [out(0, AT_U, D), out(1, AT_Q, 2 * HD), out(2, AT_V, HD)]
    order = order_matrix()
    for copy in copies[:4]:
        copy.wait()
    first = core_ref[0] == 0
    mine, theirs = [], []
    for line in range(LINES):
        a = up[:, (2 * line) * COLS : (2 * line + 1) * COLS]
        b = up[:, (2 * line + 1) * COLS : (2 * line + 2) * COLS]
        mine.append(jnp.where(first, a, b))
        theirs.append(jnp.where(first, b, a))
    packed[:, :, AT_U : AT_U + D] = spread(jnp.concatenate(mine + theirs, axis=1))
    outs[0].start()
    for n, at in enumerate((AT_Q, AT_K, AT_V)):
        copies[4 + 2 * n].wait()
        copies[5 + 2 * n].wait()
        packed[:, :, at : at + HD] = spread(dot(feats[n], order, TN, BF16))
        if n > 0:
            outs[n].start()
    for copy in outs:
        copy.wait()


def weight_kernel(raw_ref, w_ref):
    pick = iota((SOURCES, TOKENS), 1) - PAIR * iota((SOURCES, TOKENS), 0)
    for b in range(LINES):
        block = raw_ref[b * SOURCES : (b + 1) * SOURCES].reshape(TOKENS, W_LANES)
        for j in range(PAIR):
            part = dot((pick == j).astype(BF16), block, NN, BF16)
            for i in range(SPLIT * j, min(SPLIT * (j + 1), ROWS)):
                lane = (i - SPLIT * j) * COLS
                w_ref[i * SOURCES : (i + 1) * SOURCES, b * COLS : (b + 1) * COLS] = part[
                    :, lane : lane + COLS
                ]


def rows_of(x_ref, at, lanes):
    return x_ref[:, :, at : at + lanes].reshape(TOKENS, lanes)


def scale_upstream(x_ref, gate_ref):
    return (gate_ref[...] * rows_of(x_ref, AT_U, D).astype(F32)).astype(BF16)


def forward_kernel(gate_ref, x_ref, probs_ref, swap_ref, mine_ref):
    q, k, v = (rows_of(x_ref, at, HD) for at in (AT_Q, AT_K, AT_V))
    factor = 1.0 / jnp.sqrt(F32(HEAD))
    same = ((iota((TOKENS, TOKENS), 0) ^ iota((TOKENS, TOKENS), 1)) & 1) == 0
    low, v_rows = [], []
    for h in range(HEADS):
        mask = head_mask(h)
        scores = dot(q * mask, k, NT) * factor
        scores = jnp.where(same, scores, -jnp.inf)
        expd = jnp.exp(scores - jnp.max(scores, axis=-1, keepdims=True))
        probs = expd / jnp.sum(expd, axis=-1, keepdims=True)
        probs_ref[h] = probs
        low.append(probs.astype(BF16))
        v_rows.append(v * mask)
    attended = dot(jnp.concatenate(low, axis=1), jnp.concatenate(v_rows, axis=0), NN, BF16)
    scaled = scale_upstream(x_ref, gate_ref)
    swap_ref[:, :HD] = attended
    swap_ref[:, HD:] = scaled[:, HALF:]
    mine_ref[...] = scaled[:, :HALF]


def share_kernel(line_ref, swap_ref, got_ref, mine_ref, o0_ref, o1_ref, o2_ref, o3_ref, packed):
    share = dot(swap_ref[:, :HD], mine_ref[...], TN) + dot(got_ref[:, :HD], got_ref[:, HD:], TN)
    share = share.astype(BF16)
    for b in range(LINES):
        for i in range(ROWS):
            packed[b, :, i * COLS : (i + 1) * COLS] = share[
                i * SOURCES : (i + 1) * SOURCES, b * COLS : (b + 1) * COLS
            ]
    line = line_ref[0]
    for s, ref in enumerate((o0_ref, o1_ref, o2_ref, o3_ref)):
        ref[...] = packed[lax.rem(line + s, LINES)]


def backward_kernel(gate_ref, x_ref, probs_ref, wm_ref, wt_ref, dq_ref, dk_ref, dv_ref):
    q, k, v = (rows_of(x_ref, at, HD) for at in (AT_Q, AT_K, AT_V))
    factor = 1.0 / jnp.sqrt(F32(HEAD))
    scaled = scale_upstream(x_ref, gate_ref)
    grad = dot(scaled[:, :HALF], wm_ref[...], NT) + dot(scaled[:, HALF:], wt_ref[...], NT)
    grad = grad.astype(BF16)
    low, score_grads, g_rows, q_rows, k_rows = [], [], [], [], []
    for h in range(HEADS):
        mask = head_mask(h)
        g_head = grad * mask
        probs = probs_ref[h]
        prob_grad = dot(g_head, v, NT)
        inner = jnp.sum(probs * prob_grad, axis=-1, keepdims=True)
        score_grads.append((probs * (prob_grad - inner)).astype(BF16))
        low.append(probs.astype(BF16))
        g_rows.append(g_head)
        q_rows.append(q * mask)
        k_rows.append(k * mask)
    wide = jnp.concatenate(score_grads, axis=1)
    tall = jnp.concatenate(score_grads, axis=0)
    dq_ref[...] = (dot(wide, jnp.concatenate(k_rows, axis=0), NN) * factor).astype(BF16)
    dk_ref[...] = (dot(tall, jnp.concatenate(q_rows, axis=0), TN) * factor).astype(BF16)
    dv_ref[...] = dot(jnp.concatenate(low, axis=0), jnp.concatenate(g_rows, axis=0), TN, BF16)


def sum_kernel(p0_ref, p1_ref, p2_ref, p3_ref, o_ref):
    total = sum(ref[...].astype(F32) for ref in (p0_ref, p1_ref, p2_ref, p3_ref)).astype(BF16)
    lanes = SPLIT * COLS
    pad = jnp.zeros((SOURCES, PAIR * lanes - ROWS * COLS), BF16)
    low = jnp.concatenate([total[:, lanes:], pad], axis=1)
    put = iota((TOKENS, SOURCES), 0) - PAIR * iota((TOKENS, SOURCES), 1)
    mixed = dot((put == 0).astype(BF16), total[:, :lanes], NN) + dot((put == 1).astype(BF16), low, NN)
    o_ref[...] = mixed.astype(BF16)


def back_kernel(swap_ref, dq_ref, dk_ref, dv_ref, sum_ref, x_ref):
    x_ref[:, :, :HD] = spread(swap_ref[:, :HD])
    for n, ref in enumerate((dq_ref, dk_ref, dv_ref)):
        x_ref[:, :, (n + 1) * HD : (n + 2) * HD] = spread(ref[...])
    x_ref[:, :, AT_G:OUT_LANES] = spread(sum_ref[...])


def final_kernel(
    core_ref, gate_ref, z_ref, wm_ref, wt_ref, out_ref, dq_ref, dk_ref, dv_ref, wg_ref
):
    att = rows_of(z_ref, 0, HD)
    gate = gate_ref[...]
    mine = (gate[:, :HALF] * dot(att, wm_ref[...], NN)).astype(BF16)
    theirs = (gate[:, HALF:] * dot(att, wt_ref[...], NN)).astype(BF16)
    first = core_ref[0] == 0
    parts = []
    for line in range(LINES):
        a = mine[:, line * COLS : (line + 1) * COLS]
        b = theirs[:, line * COLS : (line + 1) * COLS]
        parts += [jnp.where(first, a, b), jnp.where(first, b, a)]
    out_ref[...] = jnp.concatenate(parts, axis=1)
    order = order_matrix()
    for n, ref in enumerate((dq_ref, dk_ref, dv_ref)):
        ref[...] = dot(order, rows_of(z_ref, (n + 1) * HD, HD), NT, BF16)
    pick = ((iota((8, TOKENS), 1) & 1) == iota((8, TOKENS), 0)).astype(BF16)
    sums = dot(pick, rows_of(z_ref, AT_G, SPLIT * COLS), NN)
    for i in range(ROWS):
        j, lane = i // SPLIT, (i % SPLIT) * COLS
        wg_ref[i : i + 1, :] = sums[j : j + 1, lane : lane + COLS]


def call(kernel, outs, args, scalars=0, far=0, far_out=False, scratch=(), flops=10**8, limit=24):
    smem = [pl.BlockSpec(memory_space=pltpu.SMEM)] * scalars
    vmem = [pl.BlockSpec(memory_space=pltpu.VMEM)] * (len(args) - scalars - far)
    hbm = [pl.BlockSpec(memory_space=pltpu.HBM)] * far
    moved = sum(int(np.prod(x.shape)) * x.dtype.itemsize for x in [*args, *outs])
    single = len(outs) == 1
    out_spec = [pl.BlockSpec(memory_space=pltpu.HBM if far_out else pltpu.VMEM)] * len(outs)
    return pl.pallas_call(
        kernel,
        out_shape=outs[0] if single else outs,
        in_specs=smem + vmem + hbm,
        out_specs=out_spec[0] if single else out_spec,
        scratch_shapes=scratch,
        cost_estimate=pl.CostEstimate(flops=flops, bytes_accessed=moved, transcendentals=0),
        compiler_params=pltpu.CompilerParams(vmem_limit_bytes=limit * 1024 * 1024),
    )(*args)


def shape(*dims, kind=BF16):
    return jax.ShapeDtypeStruct(dims, kind)


def column_order():
    cols = np.arange(D).reshape(LINES, CORES, COLS)
    return [np.concatenate([cols[:, c].ravel(), cols[:, 1 - c].ravel()]) for c in range(CORES)]


def shards(queries, keys, values, out_weight, upstream, timestep):
    core = lax.axis_index("core").astype(jnp.int32)
    core_s, line_s = core.reshape(1), lax.axis_index("line").astype(jnp.int32).reshape(1)

    def shift_line(x, s):
        return lax.ppermute(x, "line", [(d, (d + s) % LINES) for d in range(LINES)])

    def swap_core(x):
        return lax.ppermute(x, "core", [(0, 1), (1, 0)])

    orders = [o.astype(np.float32) for o in column_order()]
    index = jnp.where(core == 0, orders[0], orders[1])
    freq = jnp.exp(-jnp.log(10000.0) * index / D)
    gate = (1.5 + jnp.sin(timestep.astype(F32)[0] * freq)).reshape(1, D)

    flat = [x.reshape(TOKENS, HD).T for x in (queries, keys, values)]
    sent = call(
        pack_kernel,
        [shape(SOURCES, PAIR, IN_LANES)],
        (core_s, *flat, upstream.reshape(TOKENS, D)),
        scalars=1,
        far=4,
        far_out=True,
        limit=60,
        scratch=[
            pltpu.VMEM((3, HD, TOKENS), BF16),
            pltpu.VMEM((TOKENS, D), BF16),
            pltpu.VMEM((SOURCES, PAIR, IN_LANES), BF16),
            pltpu.SemaphoreType.DMA((13,)),
        ],
    )
    w_sent = call(repeat_kernel, [shape(W_PEERS, PAIR, W_LANES)], (out_weight,))
    slab = lax.all_to_all(sent, OTHERS, split_axis=0, concat_axis=0, tiled=True)
    w_sent, _ = lax.optimization_barrier((w_sent, slab))
    w_raw = lax.all_to_all(w_sent, ("line", *OTHERS), split_axis=0, concat_axis=0, tiled=True)

    probs, swap, mine = call(
        forward_kernel,
        [shape(HEADS, TOKENS, TOKENS, kind=F32), shape(TOKENS, HD + HALF), shape(TOKENS, HALF)],
        (gate, slab),
    )
    got = swap_core(swap)
    pieces = call(
        share_kernel,
        [shape(SOURCES, ROWS * COLS)] * LINES,
        (line_s, swap, got, mine),
        scalars=1,
        scratch=[pltpu.VMEM((LINES, SOURCES, ROWS * COLS), BF16)],
    )
    sums = [pieces[0]] + [shift_line(pieces[s], s) for s in range(1, LINES)]
    w_raw, _ = lax.optimization_barrier((w_raw, pieces[0]))
    w_mine = call(weight_kernel, [shape(HD, HALF)], (w_raw,))
    w_theirs = swap_core(w_mine)
    grads = call(
        backward_kernel, [shape(TOKENS, HD)] * 3, (gate, slab, probs, w_mine, w_theirs), flops=10**9
    )
    total = call(sum_kernel, [shape(TOKENS, SPLIT * COLS)], sums, flops=10**10)
    back = call(back_kernel, [shape(SOURCES, PAIR, OUT_LANES)], (swap, *grads, total))
    frame = lax.all_to_all(back, OTHERS, split_axis=0, concat_axis=0, tiled=True)
    output, dq, dk, dv, weight_grad = call(
        final_kernel,
        [shape(TOKENS, D)] + [shape(HD, TOKENS)] * 3 + [shape(ROWS, COLS, kind=F32)],
        (core_s, gate, frame, w_mine, w_theirs),
        scalars=1,
    )
    dims = queries.shape
    return (output.reshape(upstream.shape), *(x.T.reshape(dims) for x in (dq, dk, dv)), weight_grad)


def solution(mesh):
    cut = jax.sharding.Mesh(mesh.devices.reshape(tuple(AXES.values())), tuple(AXES))
    dp, tm = ("line", "core"), OTHERS
    act = P(dp, tm, None, None)
    return jax.shard_map(
        shards,
        mesh=cut,
        in_specs=(act, act, act, P(tm, dp), act, P(dp)),
        out_specs=(act, act, act, act, P(tm, dp)),
        check_vma=False,
    )
```

```python
import jax
import jax.numpy as jnp
import numpy as np
from jax import lax
from jax.experimental import pallas as pl
from jax.experimental.pallas import tpu as pltpu
from jax.sharding import PartitionSpec as P

D = 1152
HEADS = 8
HEAD = 72
HD = HEADS * HEAD
CORES = 2
LINES = 4
SOURCES = 64
PAIR = 2
TOKENS = SOURCES * PAIR
ROWS = HD // SOURCES
COLS = D // (CORES * LINES)
HALF = D // CORES
SPLIT = (ROWS + 1) // 2
F32 = jnp.float32
BF16 = jnp.bfloat16

AXES = {"line": LINES, "core": CORES, "x": 4, "y": 2, "z": 8}
OTHERS = ("x", "y", "z")
W_LANES = ROWS * HALF // PAIR

AT_U = 0
AT_Q = AT_U + D
AT_K = AT_Q + HD
AT_V = AT_K + HD
IN_LANES = AT_V + HD
AT_G = 4 * HD
OUT_LANES = AT_G + SPLIT * COLS


def iota(shape, dim):
    return lax.broadcasted_iota(jnp.int32, shape, dim)


def order_matrix():
    feature, place = iota((HD, HD), 0), iota((HD, HD), 1)
    return (feature == ROWS * (place & (SOURCES - 1)) + (place >> 6)).astype(BF16)


def head_mask(head):
    return (((iota((1, HD), 1) & (SOURCES - 1)) >> 3) == head).astype(BF16)


def dot(a, b, dims, kind=F32):
    return lax.dot_general(a, b, (dims, ((), ())), preferred_element_type=F32).astype(kind)


NN = ((1,), (0,))
NT = ((1,), (1,))
TN = ((0,), (0,))


def spread(x):
    return x.reshape(SOURCES, PAIR, x.shape[-1])


def repeat_kernel(line_ref, w0, w1, w2, w3, x_ref, slots):
    for s, ref in enumerate((w0, w1, w2, w3)):
        slots[s, :ROWS, :] = ref[...].astype(F32)
    line = line_ref[0]
    blocks = [slots[lax.rem(line - b + LINES, LINES)] for b in range(LINES)]
    full = jnp.concatenate(blocks, axis=1)
    rows = [full[i : i + 1] for i in range(ROWS)]
    mid = ROWS // 2
    top = jnp.concatenate(rows[:mid] + [rows[mid][:, : HALF // 2]], axis=1)
    low = jnp.concatenate([rows[mid][:, HALF // 2 :]] + rows[mid + 1 :], axis=1)
    odd = (iota((TOKENS, W_LANES), 0) & 1) == 1
    x_ref[...] = spread(jnp.where(odd, low, top).astype(BF16))


def pack_kernel(core_ref, q_ref, k_ref, v_ref, u_ref, x_ref, feats, up, packed, sems):
    copies = []
    for h in range(4):
        part = pl.ds(h * (TOKENS // 4), TOKENS // 4)
        copies.append(pltpu.make_async_copy(u_ref.at[part], up.at[part], sems.at[h]))
    for n, ref in enumerate((q_ref, k_ref, v_ref)):
        for h in range(2):
            part = pl.ds(h * (HD // 2), HD // 2)
            copies.append(
                pltpu.make_async_copy(ref.at[part], feats.at[n, part], sems.at[4 + 2 * n + h])
            )
    for copy in copies:
        copy.start()

    def out(n, at, lanes):
        part = pl.ds(at, lanes)
        return pltpu.make_async_copy(
            packed.at[:, :, part], x_ref.at[:, :, part], sems.at[10 + n]
        )

    outs = [out(0, AT_U, D), out(1, AT_Q, 2 * HD), out(2, AT_V, HD)]
    order = order_matrix()
    for copy in copies[:4]:
        copy.wait()
    first = core_ref[0] == 0
    mine, theirs = [], []
    for line in range(LINES):
        a = up[:, (2 * line) * COLS : (2 * line + 1) * COLS]
        b = up[:, (2 * line + 1) * COLS : (2 * line + 2) * COLS]
        mine.append(jnp.where(first, a, b))
        theirs.append(jnp.where(first, b, a))
    packed[:, :, AT_U : AT_U + D] = spread(jnp.concatenate(mine + theirs, axis=1))
    outs[0].start()
    for n, at in enumerate((AT_Q, AT_K, AT_V)):
        copies[4 + 2 * n].wait()
        copies[5 + 2 * n].wait()
        packed[:, :, at : at + HD] = spread(dot(feats[n], order, TN, BF16))
        if n > 0:
            outs[n].start()
    for copy in outs:
        copy.wait()


def weight_kernel(raw_ref, w_ref):
    pick = iota((SOURCES, TOKENS), 1) - PAIR * iota((SOURCES, TOKENS), 0)
    raw = raw_ref[...].reshape(TOKENS, W_LANES)
    top = dot((pick == 0).astype(BF16), raw, NN, BF16)
    low = dot((pick == 1).astype(BF16), raw, NN, BF16)
    mid, part = ROWS // 2, HALF // 2
    for i in range(ROWS):
        at = slice(i * SOURCES, (i + 1) * SOURCES)
        if i < mid:
            w_ref[at, :] = top[:, i * HALF : (i + 1) * HALF]
        elif i == mid:
            w_ref[at, :part] = top[:, i * HALF :]
            w_ref[at, part:] = low[:, :part]
        else:
            w_ref[at, :] = low[:, part + (i - mid - 1) * HALF : part + (i - mid) * HALF]


def rows_of(x_ref, at, lanes):
    return x_ref[:, :, at : at + lanes].reshape(TOKENS, lanes)


def scale_upstream(x_ref, gate_ref):
    return (gate_ref[...] * rows_of(x_ref, AT_U, D).astype(F32)).astype(BF16)


def forward_kernel(gate_ref, x_ref, probs_ref, swap_ref, mine_ref):
    q, k, v = (rows_of(x_ref, at, HD) for at in (AT_Q, AT_K, AT_V))
    factor = 1.0 / jnp.sqrt(F32(HEAD))
    same = ((iota((TOKENS, TOKENS), 0) ^ iota((TOKENS, TOKENS), 1)) & 1) == 0
    low, v_rows = [], []
    for h in range(HEADS):
        mask = head_mask(h)
        scores = dot(q * mask, k, NT) * factor
        scores = jnp.where(same, scores, -jnp.inf)
        expd = jnp.exp(scores - jnp.max(scores, axis=-1, keepdims=True))
        probs = expd / jnp.sum(expd, axis=-1, keepdims=True)
        probs_ref[h] = probs
        low.append(probs.astype(BF16))
        v_rows.append(v * mask)
    attended = dot(jnp.concatenate(low, axis=1), jnp.concatenate(v_rows, axis=0), NN, BF16)
    scaled = scale_upstream(x_ref, gate_ref)
    swap_ref[:, :HD] = attended
    swap_ref[:, HD:] = scaled[:, HALF:]
    mine_ref[...] = scaled[:, :HALF]


def share_kernel(line_ref, swap_ref, got_ref, mine_ref, o0_ref, o1_ref, o2_ref, o3_ref, packed):
    share = dot(swap_ref[:, :HD], mine_ref[...], TN) + dot(got_ref[:, :HD], got_ref[:, HD:], TN)
    share = share.astype(BF16)
    for b in range(LINES):
        for i in range(ROWS):
            packed[b, :, i * COLS : (i + 1) * COLS] = share[
                i * SOURCES : (i + 1) * SOURCES, b * COLS : (b + 1) * COLS
            ]
    line = line_ref[0]
    for s, ref in enumerate((o0_ref, o1_ref, o2_ref, o3_ref)):
        ref[...] = packed[lax.rem(line + s, LINES)]


def backward_kernel(gate_ref, x_ref, probs_ref, wm_ref, wt_ref, dq_ref, dk_ref, dv_ref):
    q, k, v = (rows_of(x_ref, at, HD) for at in (AT_Q, AT_K, AT_V))
    factor = 1.0 / jnp.sqrt(F32(HEAD))
    scaled = scale_upstream(x_ref, gate_ref)
    grad = dot(scaled[:, :HALF], wm_ref[...], NT) + dot(scaled[:, HALF:], wt_ref[...], NT)
    grad = grad.astype(BF16)
    low, score_grads, g_rows, q_rows, k_rows = [], [], [], [], []
    for h in range(HEADS):
        mask = head_mask(h)
        g_head = grad * mask
        probs = probs_ref[h]
        prob_grad = dot(g_head, v, NT)
        inner = jnp.sum(probs * prob_grad, axis=-1, keepdims=True)
        score_grads.append((probs * (prob_grad - inner)).astype(BF16))
        low.append(probs.astype(BF16))
        g_rows.append(g_head)
        q_rows.append(q * mask)
        k_rows.append(k * mask)
    wide = jnp.concatenate(score_grads, axis=1)
    tall = jnp.concatenate(score_grads, axis=0)
    dq_ref[...] = (dot(wide, jnp.concatenate(k_rows, axis=0), NN) * factor).astype(BF16)
    dk_ref[...] = (dot(tall, jnp.concatenate(q_rows, axis=0), TN) * factor).astype(BF16)
    dv_ref[...] = dot(jnp.concatenate(low, axis=0), jnp.concatenate(g_rows, axis=0), TN, BF16)


def sum_kernel(p0_ref, p1_ref, p2_ref, p3_ref, o_ref):
    total = sum(ref[...].astype(F32) for ref in (p0_ref, p1_ref, p2_ref, p3_ref)).astype(BF16)
    lanes = SPLIT * COLS
    pad = jnp.zeros((SOURCES, PAIR * lanes - ROWS * COLS), BF16)
    low = jnp.concatenate([total[:, lanes:], pad], axis=1)
    put = iota((TOKENS, SOURCES), 0) - PAIR * iota((TOKENS, SOURCES), 1)
    mixed = dot((put == 0).astype(BF16), total[:, :lanes], NN) + dot((put == 1).astype(BF16), low, NN)
    o_ref[...] = mixed.astype(BF16)


def back_kernel(swap_ref, dq_ref, dk_ref, dv_ref, sum_ref, x_ref):
    x_ref[:, :, :HD] = spread(swap_ref[:, :HD])
    for n, ref in enumerate((dq_ref, dk_ref, dv_ref)):
        x_ref[:, :, (n + 1) * HD : (n + 2) * HD] = spread(ref[...])
    x_ref[:, :, AT_G:OUT_LANES] = spread(sum_ref[...])


def final_kernel(
    core_ref, gate_ref, z_ref, wm_ref, wt_ref, out_ref, dq_ref, dk_ref, dv_ref, wg_ref
):
    att = rows_of(z_ref, 0, HD)
    gate = gate_ref[...]
    mine = (gate[:, :HALF] * dot(att, wm_ref[...], NN)).astype(BF16)
    theirs = (gate[:, HALF:] * dot(att, wt_ref[...], NN)).astype(BF16)
    first = core_ref[0] == 0
    parts = []
    for line in range(LINES):
        a = mine[:, line * COLS : (line + 1) * COLS]
        b = theirs[:, line * COLS : (line + 1) * COLS]
        parts += [jnp.where(first, a, b), jnp.where(first, b, a)]
    out_ref[...] = jnp.concatenate(parts, axis=1)
    order = order_matrix()
    for n, ref in enumerate((dq_ref, dk_ref, dv_ref)):
        ref[...] = dot(order, rows_of(z_ref, (n + 1) * HD, HD), NT, BF16)
    pick = ((iota((8, TOKENS), 1) & 1) == iota((8, TOKENS), 0)).astype(BF16)
    sums = dot(pick, rows_of(z_ref, AT_G, SPLIT * COLS), NN)
    for i in range(ROWS):
        j, lane = i // SPLIT, (i % SPLIT) * COLS
        wg_ref[i : i + 1, :] = sums[j : j + 1, lane : lane + COLS]


def call(kernel, outs, args, scalars=0, far=0, far_out=False, scratch=(), flops=10**8, limit=24):
    smem = [pl.BlockSpec(memory_space=pltpu.SMEM)] * scalars
    vmem = [pl.BlockSpec(memory_space=pltpu.VMEM)] * (len(args) - scalars - far)
    hbm = [pl.BlockSpec(memory_space=pltpu.HBM)] * far
    moved = sum(int(np.prod(x.shape)) * x.dtype.itemsize for x in [*args, *outs])
    single = len(outs) == 1
    out_spec = [pl.BlockSpec(memory_space=pltpu.HBM if far_out else pltpu.VMEM)] * len(outs)
    return pl.pallas_call(
        kernel,
        out_shape=outs[0] if single else outs,
        in_specs=smem + vmem + hbm,
        out_specs=out_spec[0] if single else out_spec,
        scratch_shapes=scratch,
        cost_estimate=pl.CostEstimate(flops=flops, bytes_accessed=moved, transcendentals=0),
        compiler_params=pltpu.CompilerParams(vmem_limit_bytes=limit * 1024 * 1024),
    )(*args)


def shape(*dims, kind=BF16):
    return jax.ShapeDtypeStruct(dims, kind)


def column_order():
    cols = np.arange(D).reshape(LINES, CORES, COLS)
    return [np.concatenate([cols[:, c].ravel(), cols[:, 1 - c].ravel()]) for c in range(CORES)]


def shards(queries, keys, values, out_weight, upstream, timestep):
    core = lax.axis_index("core").astype(jnp.int32)
    core_s, line_s = core.reshape(1), lax.axis_index("line").astype(jnp.int32).reshape(1)

    def shift_line(x, s):
        return lax.ppermute(x, "line", [(d, (d + s) % LINES) for d in range(LINES)])

    def swap_core(x):
        return lax.ppermute(x, "core", [(0, 1), (1, 0)])

    orders = [o.astype(np.float32) for o in column_order()]
    index = jnp.where(core == 0, orders[0], orders[1])
    freq = jnp.exp(-jnp.log(10000.0) * index / D)
    gate = (1.5 + jnp.sin(timestep.astype(F32)[0] * freq)).reshape(1, D)

    flat = [x.reshape(TOKENS, HD).T for x in (queries, keys, values)]
    sent = call(
        pack_kernel,
        [shape(SOURCES, PAIR, IN_LANES)],
        (core_s, *flat, upstream.reshape(TOKENS, D)),
        scalars=1,
        far=4,
        far_out=True,
        limit=60,
        scratch=[
            pltpu.VMEM((3, HD, TOKENS), BF16),
            pltpu.VMEM((TOKENS, D), BF16),
            pltpu.VMEM((SOURCES, PAIR, IN_LANES), BF16),
            pltpu.SemaphoreType.DMA((13,)),
        ],
    )
    own_w, _ = lax.optimization_barrier((out_weight, sent))
    weights = [own_w] + [shift_line(own_w, s) for s in range(1, LINES)]
    slab = lax.all_to_all(sent, OTHERS, split_axis=0, concat_axis=0, tiled=True)
    w_sent = call(
        repeat_kernel,
        [shape(SOURCES, PAIR, W_LANES)],
        (line_s, *weights),
        scalars=1,
        scratch=[pltpu.VMEM((LINES, 16, COLS), F32)],
    )
    w_sent, _ = lax.optimization_barrier((w_sent, slab))
    w_raw = lax.all_to_all(w_sent, OTHERS, split_axis=0, concat_axis=0, tiled=True)

    probs, swap, mine = call(
        forward_kernel,
        [shape(HEADS, TOKENS, TOKENS, kind=F32), shape(TOKENS, HD + HALF), shape(TOKENS, HALF)],
        (gate, slab),
    )
    got = swap_core(swap)
    pieces = call(
        share_kernel,
        [shape(SOURCES, ROWS * COLS)] * LINES,
        (line_s, swap, got, mine),
        scalars=1,
        scratch=[pltpu.VMEM((LINES, SOURCES, ROWS * COLS), BF16)],
    )
    sums = [pieces[0]] + [shift_line(pieces[s], s) for s in range(1, LINES)]
    w_raw, _ = lax.optimization_barrier((w_raw, pieces[0]))
    w_mine = call(weight_kernel, [shape(HD, HALF)], (w_raw,))
    w_theirs = swap_core(w_mine)
    grads = call(
        backward_kernel, [shape(TOKENS, HD)] * 3, (gate, slab, probs, w_mine, w_theirs), flops=10**9
    )
    total = call(sum_kernel, [shape(TOKENS, SPLIT * COLS)], sums, flops=10**10)
    back = call(back_kernel, [shape(SOURCES, PAIR, OUT_LANES)], (swap, *grads, total))
    frame = lax.all_to_all(back, OTHERS, split_axis=0, concat_axis=0, tiled=True)
    output, dq, dk, dv, weight_grad = call(
        final_kernel,
        [shape(TOKENS, D)] + [shape(HD, TOKENS)] * 3 + [shape(ROWS, COLS, kind=F32)],
        (core_s, gate, frame, w_mine, w_theirs),
        scalars=1,
    )
    dims = queries.shape
    return (output.reshape(upstream.shape), *(x.T.reshape(dims) for x in (dq, dk, dv)), weight_grad)


def solution(mesh):
    cut = jax.sharding.Mesh(mesh.devices.reshape(tuple(AXES.values())), tuple(AXES))
    dp, tm = ("line", "core"), OTHERS
    act = P(dp, tm, None, None)
    return jax.shard_map(
        shards,
        mesh=cut,
        in_specs=(act, act, act, P(tm, dp), act, P(dp)),
        out_specs=(act, act, act, act, P(tm, dp)),
        check_vma=False,
    )
```

```python
import jax
import jax.numpy as jnp
import numpy as np
from jax import lax
from jax.experimental import pallas as pl
from jax.experimental.pallas import tpu as pltpu
from jax.sharding import PartitionSpec as P

D = 1152
HEADS = 8
HEAD = 72
HD = HEADS * HEAD
CORES = 2
LINES = 4
SOURCES = 64
PAIR = 2
TOKENS = SOURCES * PAIR
ROWS = HD // SOURCES
COLS = D // (CORES * LINES)
HALF = D // CORES
SPLIT = (ROWS + 1) // 2
F32 = jnp.float32
BF16 = jnp.bfloat16

AXES = {"line": LINES, "core": CORES, "x": 4, "y": 2, "z": 8}
OTHERS = ("x", "y", "z")
W_LANES = ROWS * HALF // PAIR

AT_U = 0
AT_Q = AT_U + D
AT_K = AT_Q + HD
AT_V = AT_K + HD
AT_W = AT_V + HD
IN_LANES = AT_W + W_LANES
AT_G = 4 * HD
OUT_LANES = AT_G + SPLIT * COLS


def iota(shape, dim):
    return lax.broadcasted_iota(jnp.int32, shape, dim)


def order_matrix():
    feature, place = iota((HD, HD), 0), iota((HD, HD), 1)
    return (feature == ROWS * (place & (SOURCES - 1)) + (place >> 6)).astype(BF16)


def head_mask(head):
    return (((iota((1, HD), 1) & (SOURCES - 1)) >> 3) == head).astype(BF16)


def dot(a, b, dims, kind=F32):
    return lax.dot_general(a, b, (dims, ((), ())), preferred_element_type=F32).astype(kind)


NN = ((1,), (0,))
NT = ((1,), (1,))
TN = ((0,), (0,))


def spread(x):
    return x.reshape(SOURCES, PAIR, x.shape[-1])


def pack_kernel(
    core_ref,
    line_ref,
    w0,
    w1,
    w2,
    w3,
    q_ref,
    k_ref,
    v_ref,
    u_ref,
    x_ref,
    feats,
    up,
    packed,
    slots,
    sems,
):
    copies = []
    for h in range(4):
        part = pl.ds(h * (TOKENS // 4), TOKENS // 4)
        copies.append(pltpu.make_async_copy(u_ref.at[part], up.at[part], sems.at[h]))
    for n, ref in enumerate((q_ref, k_ref, v_ref)):
        for h in range(2):
            part = pl.ds(h * (HD // 2), HD // 2)
            copies.append(
                pltpu.make_async_copy(ref.at[part], feats.at[n, part], sems.at[4 + 2 * n + h])
            )
    for copy in copies:
        copy.start()

    def out(n, at, lanes):
        part = pl.ds(at, lanes)
        return pltpu.make_async_copy(
            packed.at[:, :, part], x_ref.at[:, :, part], sems.at[10 + n]
        )

    outs = [out(0, AT_U, D), out(1, AT_Q, 2 * HD), out(2, AT_V, HD + W_LANES)]
    for s, ref in enumerate((w0, w1, w2, w3)):
        slots[s, :ROWS, :] = ref[...].astype(F32)
    line = line_ref[0]
    blocks = [slots[lax.rem(line - b + LINES, LINES)] for b in range(LINES)]
    full = jnp.concatenate(blocks, axis=1)
    rows = [full[i : i + 1] for i in range(ROWS)]
    mid = ROWS // 2
    top = jnp.concatenate(rows[:mid] + [rows[mid][:, : HALF // 2]], axis=1)
    low = jnp.concatenate([rows[mid][:, HALF // 2 :]] + rows[mid + 1 :], axis=1)
    odd = (iota((TOKENS, W_LANES), 0) & 1) == 1
    packed[:, :, AT_W:IN_LANES] = spread(jnp.where(odd, low, top).astype(BF16))
    order = order_matrix()
    for copy in copies[:4]:
        copy.wait()
    first = core_ref[0] == 0
    mine, theirs = [], []
    for line in range(LINES):
        a = up[:, (2 * line) * COLS : (2 * line + 1) * COLS]
        b = up[:, (2 * line + 1) * COLS : (2 * line + 2) * COLS]
        mine.append(jnp.where(first, a, b))
        theirs.append(jnp.where(first, b, a))
    packed[:, :, AT_U : AT_U + D] = spread(jnp.concatenate(mine + theirs, axis=1))
    outs[0].start()
    for n, at in enumerate((AT_Q, AT_K, AT_V)):
        copies[4 + 2 * n].wait()
        copies[5 + 2 * n].wait()
        packed[:, :, at : at + HD] = spread(dot(feats[n], order, TN, BF16))
        if n > 0:
            outs[n].start()
    for copy in outs:
        copy.wait()


def weight_kernel(raw_ref, w_ref):
    pick = iota((SOURCES, TOKENS), 1) - PAIR * iota((SOURCES, TOKENS), 0)
    raw = rows_of(raw_ref, AT_W, W_LANES)
    top = dot((pick == 0).astype(BF16), raw, NN, BF16)
    low = dot((pick == 1).astype(BF16), raw, NN, BF16)
    mid, part = ROWS // 2, HALF // 2
    for i in range(ROWS):
        at = slice(i * SOURCES, (i + 1) * SOURCES)
        if i < mid:
            w_ref[at, :] = top[:, i * HALF : (i + 1) * HALF]
        elif i == mid:
            w_ref[at, :part] = top[:, i * HALF :]
            w_ref[at, part:] = low[:, :part]
        else:
            w_ref[at, :] = low[:, part + (i - mid - 1) * HALF : part + (i - mid) * HALF]


def rows_of(x_ref, at, lanes):
    return x_ref[:, :, at : at + lanes].reshape(TOKENS, lanes)


def scale_upstream(x_ref, gate_ref):
    return (gate_ref[...] * rows_of(x_ref, AT_U, D).astype(F32)).astype(BF16)


def forward_kernel(gate_ref, x_ref, probs_ref, swap_ref, mine_ref):
    q, k, v = (rows_of(x_ref, at, HD) for at in (AT_Q, AT_K, AT_V))
    factor = 1.0 / jnp.sqrt(F32(HEAD))
    same = ((iota((TOKENS, TOKENS), 0) ^ iota((TOKENS, TOKENS), 1)) & 1) == 0
    low, v_rows = [], []
    for h in range(HEADS):
        mask = head_mask(h)
        scores = dot(q * mask, k, NT) * factor
        scores = jnp.where(same, scores, -jnp.inf)
        expd = jnp.exp(scores - jnp.max(scores, axis=-1, keepdims=True))
        probs = expd / jnp.sum(expd, axis=-1, keepdims=True)
        probs_ref[h] = probs
        low.append(probs.astype(BF16))
        v_rows.append(v * mask)
    attended = dot(jnp.concatenate(low, axis=1), jnp.concatenate(v_rows, axis=0), NN, BF16)
    scaled = scale_upstream(x_ref, gate_ref)
    swap_ref[:, :HD] = attended
    swap_ref[:, HD:] = scaled[:, HALF:]
    mine_ref[...] = scaled[:, :HALF]


def share_kernel(line_ref, swap_ref, got_ref, mine_ref, o0_ref, o1_ref, o2_ref, o3_ref, packed):
    share = dot(swap_ref[:, :HD], mine_ref[...], TN) + dot(got_ref[:, :HD], got_ref[:, HD:], TN)
    share = share.astype(BF16)
    for b in range(LINES):
        for i in range(ROWS):
            packed[b, :, i * COLS : (i + 1) * COLS] = share[
                i * SOURCES : (i + 1) * SOURCES, b * COLS : (b + 1) * COLS
            ]
    line = line_ref[0]
    for s, ref in enumerate((o0_ref, o1_ref, o2_ref, o3_ref)):
        ref[...] = packed[lax.rem(line + s, LINES)]


def backward_kernel(gate_ref, x_ref, probs_ref, wm_ref, wt_ref, dq_ref, dk_ref, dv_ref):
    q, k, v = (rows_of(x_ref, at, HD) for at in (AT_Q, AT_K, AT_V))
    factor = 1.0 / jnp.sqrt(F32(HEAD))
    scaled = scale_upstream(x_ref, gate_ref)
    grad = dot(scaled[:, :HALF], wm_ref[...], NT) + dot(scaled[:, HALF:], wt_ref[...], NT)
    grad = grad.astype(BF16)
    low, score_grads, g_rows, q_rows, k_rows = [], [], [], [], []
    for h in range(HEADS):
        mask = head_mask(h)
        g_head = grad * mask
        probs = probs_ref[h]
        prob_grad = dot(g_head, v, NT)
        inner = jnp.sum(probs * prob_grad, axis=-1, keepdims=True)
        score_grads.append((probs * (prob_grad - inner)).astype(BF16))
        low.append(probs.astype(BF16))
        g_rows.append(g_head)
        q_rows.append(q * mask)
        k_rows.append(k * mask)
    wide = jnp.concatenate(score_grads, axis=1)
    tall = jnp.concatenate(score_grads, axis=0)
    dq_ref[...] = (dot(wide, jnp.concatenate(k_rows, axis=0), NN) * factor).astype(BF16)
    dk_ref[...] = (dot(tall, jnp.concatenate(q_rows, axis=0), TN) * factor).astype(BF16)
    dv_ref[...] = dot(jnp.concatenate(low, axis=0), jnp.concatenate(g_rows, axis=0), TN, BF16)


def sum_kernel(p0_ref, p1_ref, p2_ref, p3_ref, o_ref):
    total = sum(ref[...].astype(F32) for ref in (p0_ref, p1_ref, p2_ref, p3_ref)).astype(BF16)
    lanes = SPLIT * COLS
    pad = jnp.zeros((SOURCES, PAIR * lanes - ROWS * COLS), BF16)
    low = jnp.concatenate([total[:, lanes:], pad], axis=1)
    put = iota((TOKENS, SOURCES), 0) - PAIR * iota((TOKENS, SOURCES), 1)
    mixed = dot((put == 0).astype(BF16), total[:, :lanes], NN) + dot((put == 1).astype(BF16), low, NN)
    o_ref[...] = mixed.astype(BF16)


def back_kernel(swap_ref, dq_ref, dk_ref, dv_ref, sum_ref, x_ref):
    x_ref[:, :, :HD] = spread(swap_ref[:, :HD])
    for n, ref in enumerate((dq_ref, dk_ref, dv_ref)):
        x_ref[:, :, (n + 1) * HD : (n + 2) * HD] = spread(ref[...])
    x_ref[:, :, AT_G:OUT_LANES] = spread(sum_ref[...])


def final_kernel(
    core_ref, gate_ref, z_ref, wm_ref, wt_ref, out_ref, dq_ref, dk_ref, dv_ref, wg_ref
):
    att = rows_of(z_ref, 0, HD)
    gate = gate_ref[...]
    mine = (gate[:, :HALF] * dot(att, wm_ref[...], NN)).astype(BF16)
    theirs = (gate[:, HALF:] * dot(att, wt_ref[...], NN)).astype(BF16)
    first = core_ref[0] == 0
    parts = []
    for line in range(LINES):
        a = mine[:, line * COLS : (line + 1) * COLS]
        b = theirs[:, line * COLS : (line + 1) * COLS]
        parts += [jnp.where(first, a, b), jnp.where(first, b, a)]
    out_ref[...] = jnp.concatenate(parts, axis=1)
    order = order_matrix()
    for n, ref in enumerate((dq_ref, dk_ref, dv_ref)):
        ref[...] = dot(order, rows_of(z_ref, (n + 1) * HD, HD), NT, BF16)
    pick = ((iota((8, TOKENS), 1) & 1) == iota((8, TOKENS), 0)).astype(BF16)
    sums = dot(pick, rows_of(z_ref, AT_G, SPLIT * COLS), NN)
    for i in range(ROWS):
        j, lane = i // SPLIT, (i % SPLIT) * COLS
        wg_ref[i : i + 1, :] = sums[j : j + 1, lane : lane + COLS]


def call(kernel, outs, args, scalars=0, far=0, far_out=False, scratch=(), flops=10**8, limit=24):
    smem = [pl.BlockSpec(memory_space=pltpu.SMEM)] * scalars
    vmem = [pl.BlockSpec(memory_space=pltpu.VMEM)] * (len(args) - scalars - far)
    hbm = [pl.BlockSpec(memory_space=pltpu.HBM)] * far
    moved = sum(int(np.prod(x.shape)) * x.dtype.itemsize for x in [*args, *outs])
    single = len(outs) == 1
    out_spec = [pl.BlockSpec(memory_space=pltpu.HBM if far_out else pltpu.VMEM)] * len(outs)
    return pl.pallas_call(
        kernel,
        out_shape=outs[0] if single else outs,
        in_specs=smem + vmem + hbm,
        out_specs=out_spec[0] if single else out_spec,
        scratch_shapes=scratch,
        cost_estimate=pl.CostEstimate(flops=flops, bytes_accessed=moved, transcendentals=0),
        compiler_params=pltpu.CompilerParams(vmem_limit_bytes=limit * 1024 * 1024),
    )(*args)


def shape(*dims, kind=BF16):
    return jax.ShapeDtypeStruct(dims, kind)


def column_order():
    cols = np.arange(D).reshape(LINES, CORES, COLS)
    return [np.concatenate([cols[:, c].ravel(), cols[:, 1 - c].ravel()]) for c in range(CORES)]


def shards(queries, keys, values, out_weight, upstream, timestep):
    core = lax.axis_index("core").astype(jnp.int32)
    core_s, line_s = core.reshape(1), lax.axis_index("line").astype(jnp.int32).reshape(1)

    def shift_line(x, s):
        return lax.ppermute(x, "line", [(d, (d + s) % LINES) for d in range(LINES)])

    def swap_core(x):
        return lax.ppermute(x, "core", [(0, 1), (1, 0)])

    orders = [o.astype(np.float32) for o in column_order()]
    index = jnp.where(core == 0, orders[0], orders[1])
    freq = jnp.exp(-jnp.log(10000.0) * index / D)
    gate = (1.5 + jnp.sin(timestep.astype(F32)[0] * freq)).reshape(1, D)

    flat = [x.reshape(TOKENS, HD).T for x in (queries, keys, values)]
    weights = [out_weight] + [shift_line(out_weight, s) for s in range(1, LINES)]
    sent = call(
        pack_kernel,
        [shape(SOURCES, PAIR, IN_LANES)],
        (core_s, line_s, *weights, *flat, upstream.reshape(TOKENS, D)),
        scalars=2,
        far=4,
        far_out=True,
        limit=60,
        scratch=[
            pltpu.VMEM((3, HD, TOKENS), BF16),
            pltpu.VMEM((TOKENS, D), BF16),
            pltpu.VMEM((SOURCES, PAIR, IN_LANES), BF16),
            pltpu.VMEM((LINES, 16, COLS), F32),
            pltpu.SemaphoreType.DMA((13,)),
        ],
    )
    slab = lax.all_to_all(sent, OTHERS, split_axis=0, concat_axis=0, tiled=True)

    probs, swap, mine = call(
        forward_kernel,
        [shape(HEADS, TOKENS, TOKENS, kind=F32), shape(TOKENS, HD + HALF), shape(TOKENS, HALF)],
        (gate, slab),
    )
    got = swap_core(swap)
    pieces = call(
        share_kernel,
        [shape(SOURCES, ROWS * COLS)] * LINES,
        (line_s, swap, got, mine),
        scalars=1,
        scratch=[pltpu.VMEM((LINES, SOURCES, ROWS * COLS), BF16)],
    )
    sums = [pieces[0]] + [shift_line(pieces[s], s) for s in range(1, LINES)]
    w_mine = call(weight_kernel, [shape(HD, HALF)], (slab,))
    w_theirs = swap_core(w_mine)
    grads = call(
        backward_kernel, [shape(TOKENS, HD)] * 3, (gate, slab, probs, w_mine, w_theirs), flops=10**9
    )
    total = call(sum_kernel, [shape(TOKENS, SPLIT * COLS)], sums, flops=10**10)
    back = call(back_kernel, [shape(SOURCES, PAIR, OUT_LANES)], (swap, *grads, total))
    frame = lax.all_to_all(back, OTHERS, split_axis=0, concat_axis=0, tiled=True)
    output, dq, dk, dv, weight_grad = call(
        final_kernel,
        [shape(TOKENS, D)] + [shape(HD, TOKENS)] * 3 + [shape(ROWS, COLS, kind=F32)],
        (core_s, gate, frame, w_mine, w_theirs),
        scalars=1,
    )
    dims = queries.shape
    return (output.reshape(upstream.shape), *(x.T.reshape(dims) for x in (dq, dk, dv)), weight_grad)


def solution(mesh):
    cut = jax.sharding.Mesh(mesh.devices.reshape(tuple(AXES.values())), tuple(AXES))
    dp, tm = ("line", "core"), OTHERS
    act = P(dp, tm, None, None)
    return jax.shard_map(
        shards,
        mesh=cut,
        in_specs=(act, act, act, P(tm, dp), act, P(dp)),
        out_specs=(act, act, act, act, P(tm, dp)),
        check_vma=False,
    )
```

```python
import jax
import jax.numpy as jnp
import numpy as np
from jax import lax
from jax.experimental import pallas as pl
from jax.experimental.pallas import tpu as pltpu
from jax.sharding import PartitionSpec as P

D = 1152
HEADS = 8
HEAD = 72
HD = HEADS * HEAD
CORES = 2
LINES = 4
SOURCES = 64
PAIR = 2
TOKENS = SOURCES * PAIR
ROWS = HD // SOURCES
COLS = D // (CORES * LINES)
HALF = D // CORES
SPLIT = (ROWS + 1) // 2
F32 = jnp.float32
BF16 = jnp.bfloat16

AXES = {"line": LINES, "core": CORES, "x": 4, "y": 2, "z": 8}
OTHERS = ("x", "y", "z")
W_LANES = ROWS * HALF // PAIR

AT_U = 0
AT_Q = AT_U + D
AT_K = AT_Q + HD
AT_V = AT_K + HD
IN_LANES = AT_V + HD
AT_G = 4 * HD
OUT_LANES = AT_G + SPLIT * COLS


def iota(shape, dim):
    return lax.broadcasted_iota(jnp.int32, shape, dim)


def order_matrix():
    feature, place = iota((HD, HD), 0), iota((HD, HD), 1)
    return (feature == ROWS * (place & (SOURCES - 1)) + (place >> 6)).astype(BF16)


def head_mask(head):
    return (((iota((1, HD), 1) & (SOURCES - 1)) >> 3) == head).astype(BF16)


def dot(a, b, dims, kind=F32):
    return lax.dot_general(a, b, (dims, ((), ())), preferred_element_type=F32).astype(kind)


NN = ((1,), (0,))
NT = ((1,), (1,))
TN = ((0,), (0,))


def spread(x):
    return x.reshape(SOURCES, PAIR, x.shape[-1])


def repeat_kernel(line_ref, w0, w1, w2, w3, x_ref, slots):
    for s, ref in enumerate((w0, w1, w2, w3)):
        slots[s, :ROWS, :] = ref[...].astype(F32)
    line = line_ref[0]
    blocks = [slots[lax.rem(line - b + LINES, LINES)] for b in range(LINES)]
    full = jnp.concatenate(blocks, axis=1)
    rows = [full[i : i + 1] for i in range(ROWS)]
    mid = ROWS // 2
    top = jnp.concatenate(rows[:mid] + [rows[mid][:, : HALF // 2]], axis=1)
    low = jnp.concatenate([rows[mid][:, HALF // 2 :]] + rows[mid + 1 :], axis=1)
    odd = (iota((TOKENS, W_LANES), 0) & 1) == 1
    x_ref[...] = spread(jnp.where(odd, low, top).astype(BF16))


def pack_kernel(core_ref, q_ref, k_ref, v_ref, u_ref, x_ref, feats, up, packed, sems):
    copies = []
    for h in range(4):
        part = pl.ds(h * (TOKENS // 4), TOKENS // 4)
        copies.append(pltpu.make_async_copy(u_ref.at[part], up.at[part], sems.at[h]))
    for n, ref in enumerate((q_ref, k_ref, v_ref)):
        for h in range(2):
            part = pl.ds(h * (HD // 2), HD // 2)
            copies.append(
                pltpu.make_async_copy(ref.at[part], feats.at[n, part], sems.at[4 + 2 * n + h])
            )
    for copy in copies:
        copy.start()

    def out(n, at, lanes):
        part = pl.ds(at, lanes)
        return pltpu.make_async_copy(
            packed.at[:, :, part], x_ref.at[:, :, part], sems.at[10 + n]
        )

    outs = [out(0, AT_U, D), out(1, AT_Q, 2 * HD), out(2, AT_V, HD)]
    order = order_matrix()
    for copy in copies[:4]:
        copy.wait()
    first = core_ref[0] == 0
    mine, theirs = [], []
    for line in range(LINES):
        a = up[:, (2 * line) * COLS : (2 * line + 1) * COLS]
        b = up[:, (2 * line + 1) * COLS : (2 * line + 2) * COLS]
        mine.append(jnp.where(first, a, b))
        theirs.append(jnp.where(first, b, a))
    packed[:, :, AT_U : AT_U + D] = spread(jnp.concatenate(mine + theirs, axis=1))
    outs[0].start()
    for n, at in enumerate((AT_Q, AT_K, AT_V)):
        copies[4 + 2 * n].wait()
        copies[5 + 2 * n].wait()
        packed[:, :, at : at + HD] = spread(dot(feats[n], order, TN, BF16))
        if n > 0:
            outs[n].start()
    for copy in outs:
        copy.wait()


def weight_kernel(raw_ref, w_ref):
    pick = iota((SOURCES, TOKENS), 1) - PAIR * iota((SOURCES, TOKENS), 0)
    raw = raw_ref[...].reshape(TOKENS, W_LANES)
    top = dot((pick == 0).astype(BF16), raw, NN, BF16)
    low = dot((pick == 1).astype(BF16), raw, NN, BF16)
    mid, part = ROWS // 2, HALF // 2
    for i in range(ROWS):
        at = slice(i * SOURCES, (i + 1) * SOURCES)
        if i < mid:
            w_ref[at, :] = top[:, i * HALF : (i + 1) * HALF]
        elif i == mid:
            w_ref[at, :part] = top[:, i * HALF :]
            w_ref[at, part:] = low[:, :part]
        else:
            w_ref[at, :] = low[:, part + (i - mid - 1) * HALF : part + (i - mid) * HALF]


def rows_of(x_ref, at, lanes):
    return x_ref[:, :, at : at + lanes].reshape(TOKENS, lanes)


def scale_upstream(x_ref, gate_ref):
    return (gate_ref[...] * rows_of(x_ref, AT_U, D).astype(F32)).astype(BF16)


def forward_kernel(gate_ref, x_ref, probs_ref, swap_ref, mine_ref):
    q, k, v = (rows_of(x_ref, at, HD) for at in (AT_Q, AT_K, AT_V))
    factor = 1.0 / jnp.sqrt(F32(HEAD))
    same = ((iota((TOKENS, TOKENS), 0) ^ iota((TOKENS, TOKENS), 1)) & 1) == 0
    low, v_rows = [], []
    for h in range(HEADS):
        mask = head_mask(h)
        scores = dot(q * mask, k, NT) * factor
        scores = jnp.where(same, scores, -jnp.inf)
        expd = jnp.exp(scores - jnp.max(scores, axis=-1, keepdims=True))
        probs = expd / jnp.sum(expd, axis=-1, keepdims=True)
        probs_ref[h] = probs
        low.append(probs.astype(BF16))
        v_rows.append(v * mask)
    attended = dot(jnp.concatenate(low, axis=1), jnp.concatenate(v_rows, axis=0), NN, BF16)
    scaled = scale_upstream(x_ref, gate_ref)
    swap_ref[:, :HD] = attended
    swap_ref[:, HD:] = scaled[:, HALF:]
    mine_ref[...] = scaled[:, :HALF]


def share_kernel(line_ref, swap_ref, got_ref, mine_ref, o0_ref, o1_ref, o2_ref, o3_ref, packed):
    share = dot(swap_ref[:, :HD], mine_ref[...], TN) + dot(got_ref[:, :HD], got_ref[:, HD:], TN)
    share = share.astype(BF16)
    for b in range(LINES):
        for i in range(ROWS):
            packed[b, :, i * COLS : (i + 1) * COLS] = share[
                i * SOURCES : (i + 1) * SOURCES, b * COLS : (b + 1) * COLS
            ]
    line = line_ref[0]
    for s, ref in enumerate((o0_ref, o1_ref, o2_ref, o3_ref)):
        ref[...] = packed[lax.rem(line + s, LINES)]


def backward_kernel(gate_ref, x_ref, probs_ref, wm_ref, wt_ref, dq_ref, dk_ref, dv_ref):
    q, k, v = (rows_of(x_ref, at, HD) for at in (AT_Q, AT_K, AT_V))
    factor = 1.0 / jnp.sqrt(F32(HEAD))
    scaled = scale_upstream(x_ref, gate_ref)
    grad = dot(scaled[:, :HALF], wm_ref[...], NT) + dot(scaled[:, HALF:], wt_ref[...], NT)
    grad = grad.astype(BF16)
    low, score_grads, g_rows, q_rows, k_rows = [], [], [], [], []
    for h in range(HEADS):
        mask = head_mask(h)
        g_head = grad * mask
        probs = probs_ref[h]
        prob_grad = dot(g_head, v, NT)
        inner = jnp.sum(probs * prob_grad, axis=-1, keepdims=True)
        score_grads.append((probs * (prob_grad - inner)).astype(BF16))
        low.append(probs.astype(BF16))
        g_rows.append(g_head)
        q_rows.append(q * mask)
        k_rows.append(k * mask)
    wide = jnp.concatenate(score_grads, axis=1)
    tall = jnp.concatenate(score_grads, axis=0)
    dq_ref[...] = (dot(wide, jnp.concatenate(k_rows, axis=0), NN) * factor).astype(BF16)
    dk_ref[...] = (dot(tall, jnp.concatenate(q_rows, axis=0), TN) * factor).astype(BF16)
    dv_ref[...] = dot(jnp.concatenate(low, axis=0), jnp.concatenate(g_rows, axis=0), TN, BF16)


def sum_kernel(p0_ref, p1_ref, p2_ref, p3_ref, o_ref):
    total = sum(ref[...].astype(F32) for ref in (p0_ref, p1_ref, p2_ref, p3_ref)).astype(BF16)
    lanes = SPLIT * COLS
    pad = jnp.zeros((SOURCES, PAIR * lanes - ROWS * COLS), BF16)
    low = jnp.concatenate([total[:, lanes:], pad], axis=1)
    put = iota((TOKENS, SOURCES), 0) - PAIR * iota((TOKENS, SOURCES), 1)
    mixed = dot((put == 0).astype(BF16), total[:, :lanes], NN) + dot((put == 1).astype(BF16), low, NN)
    o_ref[...] = mixed.astype(BF16)


def back_kernel(swap_ref, dq_ref, dk_ref, dv_ref, sum_ref, x_ref):
    x_ref[:, :, :HD] = spread(swap_ref[:, :HD])
    for n, ref in enumerate((dq_ref, dk_ref, dv_ref)):
        x_ref[:, :, (n + 1) * HD : (n + 2) * HD] = spread(ref[...])
    x_ref[:, :, AT_G:OUT_LANES] = spread(sum_ref[...])


def final_kernel(
    core_ref, gate_ref, z_ref, wm_ref, wt_ref, out_ref, dq_ref, dk_ref, dv_ref, wg_ref
):
    att = rows_of(z_ref, 0, HD)
    gate = gate_ref[...]
    mine = (gate[:, :HALF] * dot(att, wm_ref[...], NN)).astype(BF16)
    theirs = (gate[:, HALF:] * dot(att, wt_ref[...], NN)).astype(BF16)
    first = core_ref[0] == 0
    parts = []
    for line in range(LINES):
        a = mine[:, line * COLS : (line + 1) * COLS]
        b = theirs[:, line * COLS : (line + 1) * COLS]
        parts += [jnp.where(first, a, b), jnp.where(first, b, a)]
    out_ref[...] = jnp.concatenate(parts, axis=1)
    order = order_matrix()
    for n, ref in enumerate((dq_ref, dk_ref, dv_ref)):
        ref[...] = dot(order, rows_of(z_ref, (n + 1) * HD, HD), NT, BF16)
    pick = ((iota((8, TOKENS), 1) & 1) == iota((8, TOKENS), 0)).astype(BF16)
    sums = dot(pick, rows_of(z_ref, AT_G, SPLIT * COLS), NN)
    for i in range(ROWS):
        j, lane = i // SPLIT, (i % SPLIT) * COLS
        wg_ref[i : i + 1, :] = sums[j : j + 1, lane : lane + COLS]


def call(kernel, outs, args, scalars=0, far=0, far_out=False, scratch=(), flops=10**8, limit=24):
    smem = [pl.BlockSpec(memory_space=pltpu.SMEM)] * scalars
    vmem = [pl.BlockSpec(memory_space=pltpu.VMEM)] * (len(args) - scalars - far)
    hbm = [pl.BlockSpec(memory_space=pltpu.HBM)] * far
    moved = sum(int(np.prod(x.shape)) * x.dtype.itemsize for x in [*args, *outs])
    single = len(outs) == 1
    out_spec = [pl.BlockSpec(memory_space=pltpu.HBM if far_out else pltpu.VMEM)] * len(outs)
    return pl.pallas_call(
        kernel,
        out_shape=outs[0] if single else outs,
        in_specs=smem + vmem + hbm,
        out_specs=out_spec[0] if single else out_spec,
        scratch_shapes=scratch,
        cost_estimate=pl.CostEstimate(flops=flops, bytes_accessed=moved, transcendentals=0),
        compiler_params=pltpu.CompilerParams(vmem_limit_bytes=limit * 1024 * 1024),
    )(*args)


def shape(*dims, kind=BF16):
    return jax.ShapeDtypeStruct(dims, kind)


def column_order():
    cols = np.arange(D).reshape(LINES, CORES, COLS)
    return [np.concatenate([cols[:, c].ravel(), cols[:, 1 - c].ravel()]) for c in range(CORES)]


def shards(queries, keys, values, out_weight, upstream, timestep):
    core = lax.axis_index("core").astype(jnp.int32)
    core_s, line_s = core.reshape(1), lax.axis_index("line").astype(jnp.int32).reshape(1)

    def shift_line(x, s):
        return lax.ppermute(x, "line", [(d, (d + s) % LINES) for d in range(LINES)])

    def swap_core(x):
        return lax.ppermute(x, "core", [(0, 1), (1, 0)])

    orders = [o.astype(np.float32) for o in column_order()]
    index = jnp.where(core == 0, orders[0], orders[1])
    freq = jnp.exp(-jnp.log(10000.0) * index / D)
    gate = (1.5 + jnp.sin(timestep.astype(F32)[0] * freq)).reshape(1, D)

    flat = [x.reshape(TOKENS, HD).T for x in (queries, keys, values)]
    sent = call(
        pack_kernel,
        [shape(SOURCES, PAIR, IN_LANES)],
        (core_s, *flat, upstream.reshape(TOKENS, D)),
        scalars=1,
        far=4,
        far_out=True,
        limit=60,
        scratch=[
            pltpu.VMEM((3, HD, TOKENS), BF16),
            pltpu.VMEM((TOKENS, D), BF16),
            pltpu.VMEM((SOURCES, PAIR, IN_LANES), BF16),
            pltpu.SemaphoreType.DMA((13,)),
        ],
    )
    own_w, _ = lax.optimization_barrier((out_weight, sent))
    weights = [own_w] + [shift_line(own_w, s) for s in range(1, LINES)]
    slab = lax.all_to_all(sent, OTHERS, split_axis=0, concat_axis=0, tiled=True)
    probs, swap, mine = call(
        forward_kernel,
        [shape(HEADS, TOKENS, TOKENS, kind=F32), shape(TOKENS, HD + HALF), shape(TOKENS, HALF)],
        (gate, slab),
    )
    got = swap_core(swap)
    *late, _ = lax.optimization_barrier((*weights, swap))
    w_sent = call(
        repeat_kernel,
        [shape(SOURCES, PAIR, W_LANES)],
        (line_s, *late),
        scalars=1,
        scratch=[pltpu.VMEM((LINES, 16, COLS), F32)],
    )
    w_raw = lax.all_to_all(w_sent, OTHERS, split_axis=0, concat_axis=0, tiled=True)
    pieces = call(
        share_kernel,
        [shape(SOURCES, ROWS * COLS)] * LINES,
        (line_s, swap, got, mine),
        scalars=1,
        scratch=[pltpu.VMEM((LINES, SOURCES, ROWS * COLS), BF16)],
    )
    sums = [pieces[0]] + [shift_line(pieces[s], s) for s in range(1, LINES)]
    w_raw, _ = lax.optimization_barrier((w_raw, pieces[0]))
    w_mine = call(weight_kernel, [shape(HD, HALF)], (w_raw,))
    w_theirs = swap_core(w_mine)
    grads = call(
        backward_kernel, [shape(TOKENS, HD)] * 3, (gate, slab, probs, w_mine, w_theirs), flops=10**9
    )
    total = call(sum_kernel, [shape(TOKENS, SPLIT * COLS)], sums, flops=10**10)
    back = call(back_kernel, [shape(SOURCES, PAIR, OUT_LANES)], (swap, *grads, total))
    frame = lax.all_to_all(back, OTHERS, split_axis=0, concat_axis=0, tiled=True)
    output, dq, dk, dv, weight_grad = call(
        final_kernel,
        [shape(TOKENS, D)] + [shape(HD, TOKENS)] * 3 + [shape(ROWS, COLS, kind=F32)],
        (core_s, gate, frame, w_mine, w_theirs),
        scalars=1,
    )
    dims = queries.shape
    return (output.reshape(upstream.shape), *(x.T.reshape(dims) for x in (dq, dk, dv)), weight_grad)


def solution(mesh):
    cut = jax.sharding.Mesh(mesh.devices.reshape(tuple(AXES.values())), tuple(AXES))
    dp, tm = ("line", "core"), OTHERS
    act = P(dp, tm, None, None)
    return jax.shard_map(
        shards,
        mesh=cut,
        in_specs=(act, act, act, P(tm, dp), act, P(dp)),
        out_specs=(act, act, act, act, P(tm, dp)),
        check_vma=False,
    )
```

```python
import jax
import jax.numpy as jnp
import numpy as np
from jax import lax
from jax.experimental import pallas as pl
from jax.experimental.pallas import tpu as pltpu
from jax.sharding import PartitionSpec as P

D = 1152
HEADS = 8
HEAD = 72
HD = HEADS * HEAD
CORES = 2
LINES = 4
SOURCES = 64
PAIR = 2
TOKENS = SOURCES * PAIR
ROWS = HD // SOURCES
COLS = D // (CORES * LINES)
HALF = D // CORES
SPLIT = (ROWS + 1) // 2
F32 = jnp.float32
BF16 = jnp.bfloat16

AXES = {"line": LINES, "core": CORES, "x": 4, "y": 2, "z": 8}
OTHERS = ("x", "y", "z")
W_LANES = 768

AT_U = W_LANES
AT_Q = AT_U + D
AT_K = AT_Q + HD
AT_V = AT_K + HD
IN_LANES = AT_V + HD
AT_G = 4 * HD
OUT_LANES = AT_G + SPLIT * COLS


def iota(shape, dim):
    return lax.broadcasted_iota(jnp.int32, shape, dim)


def order_matrix():
    feature, place = iota((HD, HD), 0), iota((HD, HD), 1)
    return (feature == ROWS * (place & (SOURCES - 1)) + (place >> 6)).astype(BF16)


def head_mask(head):
    return (((iota((1, HD), 1) & (SOURCES - 1)) >> 3) == head).astype(BF16)


def dot(a, b, dims, kind=F32):
    return lax.dot_general(a, b, (dims, ((), ())), preferred_element_type=F32).astype(kind)


NN = ((1,), (0,))
NT = ((1,), (1,))
TN = ((0,), (0,))


def spread(x):
    return x.reshape(SOURCES, PAIR, x.shape[-1])


def pack_kernel(
    core_ref, w_ref, q_ref, k_ref, v_ref, u_ref, x_ref, feats, up, packed, sems
):
    copies = []
    for h in range(4):
        part = pl.ds(h * (TOKENS // 4), TOKENS // 4)
        copies.append(pltpu.make_async_copy(u_ref.at[part], up.at[part], sems.at[h]))
    for n, ref in enumerate((q_ref, k_ref, v_ref)):
        for h in range(2):
            part = pl.ds(h * (HD // 2), HD // 2)
            copies.append(
                pltpu.make_async_copy(ref.at[part], feats.at[n, part], sems.at[4 + 2 * n + h])
            )
    for copy in copies:
        copy.start()

    def out(n, at, lanes):
        part = pl.ds(at, lanes)
        return pltpu.make_async_copy(
            packed.at[:, :, part], x_ref.at[:, :, part], sems.at[10 + n]
        )

    outs = [out(0, 0, AT_Q), out(1, AT_Q, 2 * HD), out(2, AT_V, HD)]
    w = w_ref[...].astype(F32)
    rows = [w[i : i + 1] for i in range(ROWS)]
    pair = []
    for j in range(PAIR):
        part = rows[SPLIT * j : SPLIT * (j + 1)]
        pad = jnp.zeros((1, W_LANES - len(part) * COLS), F32)
        pair.append(jnp.concatenate(part + [pad], axis=1))
    odd = (iota((TOKENS, W_LANES), 0) & 1) == 1
    packed[:, :, :W_LANES] = spread(jnp.where(odd, pair[1], pair[0]).astype(BF16))
    order = order_matrix()
    for copy in copies[:4]:
        copy.wait()
    first = core_ref[0] == 0
    mine, theirs = [], []
    for line in range(LINES):
        a = up[:, (2 * line) * COLS : (2 * line + 1) * COLS]
        b = up[:, (2 * line + 1) * COLS : (2 * line + 2) * COLS]
        mine.append(jnp.where(first, a, b))
        theirs.append(jnp.where(first, b, a))
    packed[:, :, AT_U : AT_U + D] = spread(jnp.concatenate(mine + theirs, axis=1))
    outs[0].start()
    for n, at in enumerate((AT_Q, AT_K, AT_V)):
        copies[4 + 2 * n].wait()
        copies[5 + 2 * n].wait()
        packed[:, :, at : at + HD] = spread(dot(feats[n], order, TN, BF16))
        if n > 0:
            outs[n].start()
    for copy in outs:
        copy.wait()


def weight_kernel(first_ref, own_ref, r1_ref, r2_ref, r3_ref, w_ref, raw):
    for s, ref in enumerate((own_ref, r1_ref, r2_ref, r3_ref)):
        raw[s] = ref[...].reshape(TOKENS, W_LANES)
    first = first_ref[0]
    pick = iota((SOURCES, TOKENS), 1) - PAIR * iota((SOURCES, TOKENS), 0)
    for b in range(LINES):
        block = raw[lax.rem(first - b + LINES, LINES)]
        for j in range(PAIR):
            part = dot((pick == j).astype(BF16), block, NN, BF16)
            for i in range(SPLIT * j, min(SPLIT * (j + 1), ROWS)):
                lane = (i - SPLIT * j) * COLS
                w_ref[i * SOURCES : (i + 1) * SOURCES, b * COLS : (b + 1) * COLS] = part[
                    :, lane : lane + COLS
                ]


def rows_of(x_ref, at, lanes):
    return x_ref[:, :, at : at + lanes].reshape(TOKENS, lanes)


def scale_upstream(x_ref, gate_ref):
    return (gate_ref[...] * rows_of(x_ref, AT_U, D).astype(F32)).astype(BF16)


def forward_kernel(gate_ref, x_ref, probs_ref, swap_ref, mine_ref):
    q, k, v = (rows_of(x_ref, at, HD) for at in (AT_Q, AT_K, AT_V))
    factor = 1.0 / jnp.sqrt(F32(HEAD))
    same = ((iota((TOKENS, TOKENS), 0) ^ iota((TOKENS, TOKENS), 1)) & 1) == 0
    low, v_rows = [], []
    for h in range(HEADS):
        mask = head_mask(h)
        scores = dot(q * mask, k, NT) * factor
        scores = jnp.where(same, scores, -jnp.inf)
        expd = jnp.exp(scores - jnp.max(scores, axis=-1, keepdims=True))
        probs = expd / jnp.sum(expd, axis=-1, keepdims=True)
        probs_ref[h] = probs
        low.append(probs.astype(BF16))
        v_rows.append(v * mask)
    attended = dot(jnp.concatenate(low, axis=1), jnp.concatenate(v_rows, axis=0), NN, BF16)
    scaled = scale_upstream(x_ref, gate_ref)
    swap_ref[:, :HD] = attended
    swap_ref[:, HD:] = scaled[:, HALF:]
    mine_ref[...] = scaled[:, :HALF]


def share_kernel(line_ref, swap_ref, got_ref, mine_ref, o0_ref, o1_ref, o2_ref, o3_ref, packed):
    share = dot(swap_ref[:, :HD], mine_ref[...], TN) + dot(got_ref[:, :HD], got_ref[:, HD:], TN)
    share = share.astype(BF16)
    for b in range(LINES):
        for i in range(ROWS):
            packed[b, :, i * COLS : (i + 1) * COLS] = share[
                i * SOURCES : (i + 1) * SOURCES, b * COLS : (b + 1) * COLS
            ]
    line = line_ref[0]
    for s, ref in enumerate((o0_ref, o1_ref, o2_ref, o3_ref)):
        ref[...] = packed[lax.rem(line + s, LINES)]


def backward_kernel(gate_ref, x_ref, probs_ref, wm_ref, wt_ref, dq_ref, dk_ref, dv_ref):
    q, k, v = (rows_of(x_ref, at, HD) for at in (AT_Q, AT_K, AT_V))
    factor = 1.0 / jnp.sqrt(F32(HEAD))
    scaled = scale_upstream(x_ref, gate_ref)
    grad = dot(scaled[:, :HALF], wm_ref[...], NT) + dot(scaled[:, HALF:], wt_ref[...], NT)
    grad = grad.astype(BF16)
    low, score_grads, g_rows, q_rows, k_rows = [], [], [], [], []
    for h in range(HEADS):
        mask = head_mask(h)
        g_head = grad * mask
        probs = probs_ref[h]
        prob_grad = dot(g_head, v, NT)
        inner = jnp.sum(probs * prob_grad, axis=-1, keepdims=True)
        score_grads.append((probs * (prob_grad - inner)).astype(BF16))
        low.append(probs.astype(BF16))
        g_rows.append(g_head)
        q_rows.append(q * mask)
        k_rows.append(k * mask)
    wide = jnp.concatenate(score_grads, axis=1)
    tall = jnp.concatenate(score_grads, axis=0)
    dq_ref[...] = (dot(wide, jnp.concatenate(k_rows, axis=0), NN) * factor).astype(BF16)
    dk_ref[...] = (dot(tall, jnp.concatenate(q_rows, axis=0), TN) * factor).astype(BF16)
    dv_ref[...] = dot(jnp.concatenate(low, axis=0), jnp.concatenate(g_rows, axis=0), TN, BF16)


def sum_kernel(p0_ref, p1_ref, p2_ref, p3_ref, o_ref):
    total = sum(ref[...].astype(F32) for ref in (p0_ref, p1_ref, p2_ref, p3_ref)).astype(BF16)
    lanes = SPLIT * COLS
    pad = jnp.zeros((SOURCES, PAIR * lanes - ROWS * COLS), BF16)
    low = jnp.concatenate([total[:, lanes:], pad], axis=1)
    put = iota((TOKENS, SOURCES), 0) - PAIR * iota((TOKENS, SOURCES), 1)
    mixed = dot((put == 0).astype(BF16), total[:, :lanes], NN) + dot((put == 1).astype(BF16), low, NN)
    o_ref[...] = mixed.astype(BF16)


def back_kernel(swap_ref, dq_ref, dk_ref, dv_ref, sum_ref, x_ref):
    x_ref[:, :, :HD] = spread(swap_ref[:, :HD])
    for n, ref in enumerate((dq_ref, dk_ref, dv_ref)):
        x_ref[:, :, (n + 1) * HD : (n + 2) * HD] = spread(ref[...])
    x_ref[:, :, AT_G:OUT_LANES] = spread(sum_ref[...])


def final_kernel(
    core_ref, gate_ref, z_ref, wm_ref, wt_ref, out_ref, dq_ref, dk_ref, dv_ref, wg_ref
):
    att = rows_of(z_ref, 0, HD)
    gate = gate_ref[...]
    mine = (gate[:, :HALF] * dot(att, wm_ref[...], NN)).astype(BF16)
    theirs = (gate[:, HALF:] * dot(att, wt_ref[...], NN)).astype(BF16)
    first = core_ref[0] == 0
    parts = []
    for line in range(LINES):
        a = mine[:, line * COLS : (line + 1) * COLS]
        b = theirs[:, line * COLS : (line + 1) * COLS]
        parts += [jnp.where(first, a, b), jnp.where(first, b, a)]
    out_ref[...] = jnp.concatenate(parts, axis=1)
    order = order_matrix()
    for n, ref in enumerate((dq_ref, dk_ref, dv_ref)):
        ref[...] = dot(order, rows_of(z_ref, (n + 1) * HD, HD), NT, BF16)
    pick = ((iota((8, TOKENS), 1) & 1) == iota((8, TOKENS), 0)).astype(BF16)
    sums = dot(pick, rows_of(z_ref, AT_G, SPLIT * COLS), NN)
    for i in range(ROWS):
        j, lane = i // SPLIT, (i % SPLIT) * COLS
        wg_ref[i : i + 1, :] = sums[j : j + 1, lane : lane + COLS]


def call(kernel, outs, args, scalars=0, far=0, far_out=False, scratch=(), flops=10**8, limit=24):
    smem = [pl.BlockSpec(memory_space=pltpu.SMEM)] * scalars
    vmem = [pl.BlockSpec(memory_space=pltpu.VMEM)] * (len(args) - scalars - far)
    hbm = [pl.BlockSpec(memory_space=pltpu.HBM)] * far
    moved = sum(int(np.prod(x.shape)) * x.dtype.itemsize for x in [*args, *outs])
    single = len(outs) == 1
    out_spec = [pl.BlockSpec(memory_space=pltpu.HBM if far_out else pltpu.VMEM)] * len(outs)
    return pl.pallas_call(
        kernel,
        out_shape=outs[0] if single else outs,
        in_specs=smem + vmem + hbm,
        out_specs=out_spec[0] if single else out_spec,
        scratch_shapes=scratch,
        cost_estimate=pl.CostEstimate(flops=flops, bytes_accessed=moved, transcendentals=0),
        compiler_params=pltpu.CompilerParams(vmem_limit_bytes=limit * 1024 * 1024),
    )(*args)


def shape(*dims, kind=BF16):
    return jax.ShapeDtypeStruct(dims, kind)


def column_order():
    cols = np.arange(D).reshape(LINES, CORES, COLS)
    return [np.concatenate([cols[:, c].ravel(), cols[:, 1 - c].ravel()]) for c in range(CORES)]


def shards(queries, keys, values, out_weight, upstream, timestep):
    core = lax.axis_index("core").astype(jnp.int32)
    core_s, line_s = core.reshape(1), lax.axis_index("line").astype(jnp.int32).reshape(1)
    first_block = (lax.axis_index("line") + lax.axis_index("x")) % LINES
    first_s = first_block.astype(jnp.int32).reshape(1)

    def shift_line(x, s):
        return lax.ppermute(x, "line", [(d, (d + s) % LINES) for d in range(LINES)])

    def step_line(x):
        size = AXES["x"]
        pairs = [
            (((a + b) % LINES) * size + b, a * size + b) for a in range(LINES) for b in range(size)
        ]
        return lax.ppermute(x, ("line", "x"), pairs)

    def shift_x(x, s):
        return lax.ppermute(x, "x", [(d, (d + s) % LINES) for d in range(LINES)])

    def swap_core(x):
        return lax.ppermute(x, "core", [(0, 1), (1, 0)])

    orders = [o.astype(np.float32) for o in column_order()]
    index = jnp.where(core == 0, orders[0], orders[1])
    freq = jnp.exp(-jnp.log(10000.0) * index / D)
    gate = (1.5 + jnp.sin(timestep.astype(F32)[0] * freq)).reshape(1, D)

    flat = [x.reshape(TOKENS, HD).T for x in (queries, keys, values)]
    sent = call(
        pack_kernel,
        [shape(SOURCES, PAIR, IN_LANES)],
        (core_s, out_weight, *flat, upstream.reshape(TOKENS, D)),
        scalars=1,
        far=4,
        far_out=True,
        limit=60,
        scratch=[
            pltpu.VMEM((3, HD, TOKENS), BF16),
            pltpu.VMEM((TOKENS, D), BF16),
            pltpu.VMEM((SOURCES, PAIR, IN_LANES), BF16),
            pltpu.SemaphoreType.DMA((13,)),
        ],
    )
    slab = lax.all_to_all(sent, OTHERS, split_axis=0, concat_axis=0, tiled=True)

    probs, swap, mine = call(
        forward_kernel,
        [shape(HEADS, TOKENS, TOKENS, kind=F32), shape(TOKENS, HD + HALF), shape(TOKENS, HALF)],
        (gate, slab),
    )
    got = swap_core(swap)
    pieces = call(
        share_kernel,
        [shape(SOURCES, ROWS * COLS)] * LINES,
        (line_s, swap, got, mine),
        scalars=1,
        scratch=[pltpu.VMEM((LINES, SOURCES, ROWS * COLS), BF16)],
    )
    sums = [pieces[0]] + [shift_line(pieces[s], s) for s in range(1, LINES)]
    raw, _ = lax.optimization_barrier((step_line(slab[:, :, :W_LANES]), pieces[0]))
    raws = [raw] + [shift_x(raw, s) for s in range(1, LINES)]
    w_mine = call(
        weight_kernel,
        [shape(HD, HALF)],
        (first_s, *raws),
        scalars=1,
        scratch=[pltpu.VMEM((LINES, TOKENS, W_LANES), BF16)],
    )
    w_theirs = swap_core(w_mine)
    grads = call(
        backward_kernel, [shape(TOKENS, HD)] * 3, (gate, slab, probs, w_mine, w_theirs), flops=10**9
    )
    total = call(sum_kernel, [shape(TOKENS, SPLIT * COLS)], sums, flops=10**10)
    back = call(back_kernel, [shape(SOURCES, PAIR, OUT_LANES)], (swap, *grads, total))
    frame = lax.all_to_all(back, OTHERS, split_axis=0, concat_axis=0, tiled=True)
    output, dq, dk, dv, weight_grad = call(
        final_kernel,
        [shape(TOKENS, D)] + [shape(HD, TOKENS)] * 3 + [shape(ROWS, COLS, kind=F32)],
        (core_s, gate, frame, w_mine, w_theirs),
        scalars=1,
    )
    dims = queries.shape
    return (output.reshape(upstream.shape), *(x.T.reshape(dims) for x in (dq, dk, dv)), weight_grad)


def solution(mesh):
    cut = jax.sharding.Mesh(mesh.devices.reshape(tuple(AXES.values())), tuple(AXES))
    dp, tm = ("line", "core"), OTHERS
    act = P(dp, tm, None, None)
    return jax.shard_map(
        shards,
        mesh=cut,
        in_specs=(act, act, act, P(tm, dp), act, P(dp)),
        out_specs=(act, act, act, act, P(tm, dp)),
        check_vma=False,
    )
```

```python
import jax
import jax.numpy as jnp
import numpy as np
from jax import lax
from jax.experimental import pallas as pl
from jax.experimental.pallas import tpu as pltpu
from jax.sharding import PartitionSpec as P

D = 1152
HEADS = 8
HEAD = 72
HD = HEADS * HEAD
CORES = 2
LINES = 4
SOURCES = 64
PAIR = 2
TOKENS = SOURCES * PAIR
ROWS = HD // SOURCES
COLS = D // (CORES * LINES)
HALF = D // CORES
SPLIT = (ROWS + 1) // 2
F32 = jnp.float32
BF16 = jnp.bfloat16

AXES = {"line": LINES, "core": CORES, "x": 4, "y": 2, "z": 8}
OTHERS = ("x", "y", "z")
W_LANES = ROWS * HALF // PAIR

AT_U = 0
AT_Q = AT_U + D
AT_K = AT_Q + HD
AT_V = AT_K + HD
IN_LANES = AT_V + HD
AT_G = 3 * HD
OUT_LANES = AT_G + SPLIT * COLS


def iota(shape, dim):
    return lax.broadcasted_iota(jnp.int32, shape, dim)


def order_matrix():
    feature, place = iota((HD, HD), 0), iota((HD, HD), 1)
    return (feature == ROWS * (place & (SOURCES - 1)) + (place >> 6)).astype(BF16)


def head_mask(head):
    return (((iota((1, HD), 1) & (SOURCES - 1)) >> 3) == head).astype(BF16)


def dot(a, b, dims, kind=F32):
    return lax.dot_general(a, b, (dims, ((), ())), preferred_element_type=F32).astype(kind)


NN = ((1,), (0,))
NT = ((1,), (1,))
TN = ((0,), (0,))


def spread(x):
    return x.reshape(SOURCES, PAIR, x.shape[-1])


def repeat_kernel(line_ref, swap_ref, w0, w1, w2, w3, x_ref, slots):
    x_ref[:, :, :HD] = spread(swap_ref[:, :HD])
    for s, ref in enumerate((w0, w1, w2, w3)):
        slots[s, :ROWS, :] = ref[...].astype(F32)
    line = line_ref[0]
    blocks = [slots[lax.rem(line - b + LINES, LINES)] for b in range(LINES)]
    full = jnp.concatenate(blocks, axis=1)
    rows = [full[i : i + 1] for i in range(ROWS)]
    mid = ROWS // 2
    top = jnp.concatenate(rows[:mid] + [rows[mid][:, : HALF // 2]], axis=1)
    low = jnp.concatenate([rows[mid][:, HALF // 2 :]] + rows[mid + 1 :], axis=1)
    odd = (iota((TOKENS, W_LANES), 0) & 1) == 1
    x_ref[:, :, HD:] = spread(jnp.where(odd, low, top).astype(BF16))


def pack_kernel(core_ref, q_ref, k_ref, v_ref, u_ref, x_ref, feats, up, packed, sems):
    copies = []
    for h in range(4):
        part = pl.ds(h * (TOKENS // 4), TOKENS // 4)
        copies.append(pltpu.make_async_copy(u_ref.at[part], up.at[part], sems.at[h]))
    for n, ref in enumerate((q_ref, k_ref, v_ref)):
        for h in range(2):
            part = pl.ds(h * (HD // 2), HD // 2)
            copies.append(
                pltpu.make_async_copy(ref.at[part], feats.at[n, part], sems.at[4 + 2 * n + h])
            )
    for copy in copies:
        copy.start()

    def out(n, at, lanes):
        part = pl.ds(at, lanes)
        return pltpu.make_async_copy(
            packed.at[:, :, part], x_ref.at[:, :, part], sems.at[10 + n]
        )

    outs = [out(0, AT_U, D), out(1, AT_Q, 2 * HD), out(2, AT_V, HD)]
    order = order_matrix()
    for copy in copies[:4]:
        copy.wait()
    first = core_ref[0] == 0
    mine, theirs = [], []
    for line in range(LINES):
        a = up[:, (2 * line) * COLS : (2 * line + 1) * COLS]
        b = up[:, (2 * line + 1) * COLS : (2 * line + 2) * COLS]
        mine.append(jnp.where(first, a, b))
        theirs.append(jnp.where(first, b, a))
    packed[:, :, AT_U : AT_U + D] = spread(jnp.concatenate(mine + theirs, axis=1))
    outs[0].start()
    for n, at in enumerate((AT_Q, AT_K, AT_V)):
        copies[4 + 2 * n].wait()
        copies[5 + 2 * n].wait()
        packed[:, :, at : at + HD] = spread(dot(feats[n], order, TN, BF16))
        if n > 0:
            outs[n].start()
    for copy in outs:
        copy.wait()


def weight_kernel(raw_ref, w_ref):
    pick = iota((SOURCES, TOKENS), 1) - PAIR * iota((SOURCES, TOKENS), 0)
    raw = rows_of(raw_ref, HD, W_LANES)
    top = dot((pick == 0).astype(BF16), raw, NN, BF16)
    low = dot((pick == 1).astype(BF16), raw, NN, BF16)
    mid, part = ROWS // 2, HALF // 2
    for i in range(ROWS):
        at = slice(i * SOURCES, (i + 1) * SOURCES)
        if i < mid:
            w_ref[at, :] = top[:, i * HALF : (i + 1) * HALF]
        elif i == mid:
            w_ref[at, :part] = top[:, i * HALF :]
            w_ref[at, part:] = low[:, :part]
        else:
            w_ref[at, :] = low[:, part + (i - mid - 1) * HALF : part + (i - mid) * HALF]


def rows_of(x_ref, at, lanes):
    return x_ref[:, :, at : at + lanes].reshape(TOKENS, lanes)


def scale_upstream(x_ref, gate_ref):
    return (gate_ref[...] * rows_of(x_ref, AT_U, D).astype(F32)).astype(BF16)


def forward_kernel(gate_ref, x_ref, probs_ref, swap_ref, mine_ref):
    q, k, v = (rows_of(x_ref, at, HD) for at in (AT_Q, AT_K, AT_V))
    factor = 1.0 / jnp.sqrt(F32(HEAD))
    same = ((iota((TOKENS, TOKENS), 0) ^ iota((TOKENS, TOKENS), 1)) & 1) == 0
    low, v_rows = [], []
    for h in range(HEADS):
        mask = head_mask(h)
        scores = dot(q * mask, k, NT) * factor
        scores = jnp.where(same, scores, -jnp.inf)
        expd = jnp.exp(scores - jnp.max(scores, axis=-1, keepdims=True))
        probs = expd / jnp.sum(expd, axis=-1, keepdims=True)
        probs_ref[h] = probs
        low.append(probs.astype(BF16))
        v_rows.append(v * mask)
    attended = dot(jnp.concatenate(low, axis=1), jnp.concatenate(v_rows, axis=0), NN, BF16)
    scaled = scale_upstream(x_ref, gate_ref)
    swap_ref[:, :HD] = attended
    swap_ref[:, HD:] = scaled[:, HALF:]
    mine_ref[...] = scaled[:, :HALF]


def share_kernel(line_ref, swap_ref, got_ref, mine_ref, o0_ref, o1_ref, o2_ref, o3_ref, packed):
    share = dot(swap_ref[:, :HD], mine_ref[...], TN) + dot(got_ref[:, :HD], got_ref[:, HD:], TN)
    share = share.astype(BF16)
    for b in range(LINES):
        for i in range(ROWS):
            packed[b, :, i * COLS : (i + 1) * COLS] = share[
                i * SOURCES : (i + 1) * SOURCES, b * COLS : (b + 1) * COLS
            ]
    line = line_ref[0]
    for s, ref in enumerate((o0_ref, o1_ref, o2_ref, o3_ref)):
        ref[...] = packed[lax.rem(line + s, LINES)]


def backward_kernel(gate_ref, x_ref, probs_ref, wm_ref, wt_ref, dq_ref, dk_ref, dv_ref):
    q, k, v = (rows_of(x_ref, at, HD) for at in (AT_Q, AT_K, AT_V))
    factor = 1.0 / jnp.sqrt(F32(HEAD))
    scaled = scale_upstream(x_ref, gate_ref)
    grad = dot(scaled[:, :HALF], wm_ref[...], NT) + dot(scaled[:, HALF:], wt_ref[...], NT)
    grad = grad.astype(BF16)
    low, score_grads, g_rows, q_rows, k_rows = [], [], [], [], []
    for h in range(HEADS):
        mask = head_mask(h)
        g_head = grad * mask
        probs = probs_ref[h]
        prob_grad = dot(g_head, v, NT)
        inner = jnp.sum(probs * prob_grad, axis=-1, keepdims=True)
        score_grads.append((probs * (prob_grad - inner)).astype(BF16))
        low.append(probs.astype(BF16))
        g_rows.append(g_head)
        q_rows.append(q * mask)
        k_rows.append(k * mask)
    wide = jnp.concatenate(score_grads, axis=1)
    tall = jnp.concatenate(score_grads, axis=0)
    dq_ref[...] = (dot(wide, jnp.concatenate(k_rows, axis=0), NN) * factor).astype(BF16)
    dk_ref[...] = (dot(tall, jnp.concatenate(q_rows, axis=0), TN) * factor).astype(BF16)
    dv_ref[...] = dot(jnp.concatenate(low, axis=0), jnp.concatenate(g_rows, axis=0), TN, BF16)


def sum_kernel(p0_ref, p1_ref, p2_ref, p3_ref, o_ref):
    total = sum(ref[...].astype(F32) for ref in (p0_ref, p1_ref, p2_ref, p3_ref)).astype(BF16)
    lanes = SPLIT * COLS
    pad = jnp.zeros((SOURCES, PAIR * lanes - ROWS * COLS), BF16)
    low = jnp.concatenate([total[:, lanes:], pad], axis=1)
    put = iota((TOKENS, SOURCES), 0) - PAIR * iota((TOKENS, SOURCES), 1)
    mixed = dot((put == 0).astype(BF16), total[:, :lanes], NN) + dot((put == 1).astype(BF16), low, NN)
    o_ref[...] = mixed.astype(BF16)


def back_kernel(dq_ref, dk_ref, dv_ref, sum_ref, x_ref):
    for n, ref in enumerate((dq_ref, dk_ref, dv_ref)):
        x_ref[:, :, n * HD : (n + 1) * HD] = spread(ref[...])
    x_ref[:, :, AT_G:OUT_LANES] = spread(sum_ref[...])


def output_kernel(core_ref, gate_ref, raw_ref, wm_ref, wt_ref, out_ref):
    att = rows_of(raw_ref, 0, HD)
    gate = gate_ref[...]
    mine = (gate[:, :HALF] * dot(att, wm_ref[...], NN)).astype(BF16)
    theirs = (gate[:, HALF:] * dot(att, wt_ref[...], NN)).astype(BF16)
    first = core_ref[0] == 0
    parts = []
    for line in range(LINES):
        a = mine[:, line * COLS : (line + 1) * COLS]
        b = theirs[:, line * COLS : (line + 1) * COLS]
        parts += [jnp.where(first, a, b), jnp.where(first, b, a)]
    out_ref[...] = jnp.concatenate(parts, axis=1)


def final_kernel(z_ref, dq_ref, dk_ref, dv_ref, wg_ref):
    order = order_matrix()
    for n, ref in enumerate((dq_ref, dk_ref, dv_ref)):
        ref[...] = dot(order, rows_of(z_ref, n * HD, HD), NT, BF16)
    pick = ((iota((8, TOKENS), 1) & 1) == iota((8, TOKENS), 0)).astype(BF16)
    sums = dot(pick, rows_of(z_ref, AT_G, SPLIT * COLS), NN)
    for i in range(ROWS):
        j, lane = i // SPLIT, (i % SPLIT) * COLS
        wg_ref[i : i + 1, :] = sums[j : j + 1, lane : lane + COLS]


def call(kernel, outs, args, scalars=0, far=0, far_out=False, scratch=(), flops=10**8, limit=24):
    smem = [pl.BlockSpec(memory_space=pltpu.SMEM)] * scalars
    vmem = [pl.BlockSpec(memory_space=pltpu.VMEM)] * (len(args) - scalars - far)
    hbm = [pl.BlockSpec(memory_space=pltpu.HBM)] * far
    moved = sum(int(np.prod(x.shape)) * x.dtype.itemsize for x in [*args, *outs])
    single = len(outs) == 1
    out_spec = [pl.BlockSpec(memory_space=pltpu.HBM if far_out else pltpu.VMEM)] * len(outs)
    return pl.pallas_call(
        kernel,
        out_shape=outs[0] if single else outs,
        in_specs=smem + vmem + hbm,
        out_specs=out_spec[0] if single else out_spec,
        scratch_shapes=scratch,
        cost_estimate=pl.CostEstimate(flops=flops, bytes_accessed=moved, transcendentals=0),
        compiler_params=pltpu.CompilerParams(vmem_limit_bytes=limit * 1024 * 1024),
    )(*args)


def shape(*dims, kind=BF16):
    return jax.ShapeDtypeStruct(dims, kind)


def column_order():
    cols = np.arange(D).reshape(LINES, CORES, COLS)
    return [np.concatenate([cols[:, c].ravel(), cols[:, 1 - c].ravel()]) for c in range(CORES)]


def shards(queries, keys, values, out_weight, upstream, timestep):
    core = lax.axis_index("core").astype(jnp.int32)
    core_s, line_s = core.reshape(1), lax.axis_index("line").astype(jnp.int32).reshape(1)

    def shift_line(x, s):
        return lax.ppermute(x, "line", [(d, (d + s) % LINES) for d in range(LINES)])

    def swap_core(x):
        return lax.ppermute(x, "core", [(0, 1), (1, 0)])

    orders = [o.astype(np.float32) for o in column_order()]
    index = jnp.where(core == 0, orders[0], orders[1])
    freq = jnp.exp(-jnp.log(10000.0) * index / D)
    gate = (1.5 + jnp.sin(timestep.astype(F32)[0] * freq)).reshape(1, D)

    flat = [x.reshape(TOKENS, HD).T for x in (queries, keys, values)]
    sent = call(
        pack_kernel,
        [shape(SOURCES, PAIR, IN_LANES)],
        (core_s, *flat, upstream.reshape(TOKENS, D)),
        scalars=1,
        far=4,
        far_out=True,
        limit=60,
        scratch=[
            pltpu.VMEM((3, HD, TOKENS), BF16),
            pltpu.VMEM((TOKENS, D), BF16),
            pltpu.VMEM((SOURCES, PAIR, IN_LANES), BF16),
            pltpu.SemaphoreType.DMA((13,)),
        ],
    )
    own_w, _ = lax.optimization_barrier((out_weight, sent))
    weights = [own_w] + [shift_line(own_w, s) for s in range(1, LINES)]
    slab = lax.all_to_all(sent, OTHERS, split_axis=0, concat_axis=0, tiled=True)
    probs, swap, mine = call(
        forward_kernel,
        [shape(HEADS, TOKENS, TOKENS, kind=F32), shape(TOKENS, HD + HALF), shape(TOKENS, HALF)],
        (gate, slab),
    )
    got = swap_core(swap)
    *late, _ = lax.optimization_barrier((*weights, swap))
    w_sent = call(
        repeat_kernel,
        [shape(SOURCES, PAIR, HD + W_LANES)],
        (line_s, swap, *late),
        scalars=1,
        scratch=[pltpu.VMEM((LINES, 16, COLS), F32)],
    )
    w_raw = lax.all_to_all(w_sent, OTHERS, split_axis=0, concat_axis=0, tiled=True)
    pieces = call(
        share_kernel,
        [shape(SOURCES, ROWS * COLS)] * LINES,
        (line_s, swap, got, mine),
        scalars=1,
        scratch=[pltpu.VMEM((LINES, SOURCES, ROWS * COLS), BF16)],
    )
    sums = [pieces[0]] + [shift_line(pieces[s], s) for s in range(1, LINES)]
    w_raw, _ = lax.optimization_barrier((w_raw, pieces[0]))
    w_mine = call(weight_kernel, [shape(HD, HALF)], (w_raw,))
    w_theirs = swap_core(w_mine)
    grads = call(
        backward_kernel, [shape(TOKENS, HD)] * 3, (gate, slab, probs, w_mine, w_theirs), flops=10**9
    )
    total = call(sum_kernel, [shape(TOKENS, SPLIT * COLS)], sums, flops=10**10)
    back = call(back_kernel, [shape(SOURCES, PAIR, OUT_LANES)], (*grads, total))
    frame = lax.all_to_all(back, OTHERS, split_axis=0, concat_axis=0, tiled=True)
    output = call(
        output_kernel, [shape(TOKENS, D)], (core_s, gate, w_raw, w_mine, w_theirs), scalars=1
    )
    dq, dk, dv, weight_grad = call(
        final_kernel, [shape(HD, TOKENS)] * 3 + [shape(ROWS, COLS, kind=F32)], (frame,)
    )
    dims = queries.shape
    return (output.reshape(upstream.shape), *(x.T.reshape(dims) for x in (dq, dk, dv)), weight_grad)


def solution(mesh):
    cut = jax.sharding.Mesh(mesh.devices.reshape(tuple(AXES.values())), tuple(AXES))
    dp, tm = ("line", "core"), OTHERS
    act = P(dp, tm, None, None)
    return jax.shard_map(
        shards,
        mesh=cut,
        in_specs=(act, act, act, P(tm, dp), act, P(dp)),
        out_specs=(act, act, act, act, P(tm, dp)),
        check_vma=False,
    )
```

```python
import jax
import jax.numpy as jnp
import numpy as np
from jax import lax
from jax.experimental import pallas as pl
from jax.experimental.pallas import tpu as pltpu
from jax.sharding import PartitionSpec as P

D = 1152
HEADS = 8
HEAD = 72
HD = HEADS * HEAD
CORES = 2
LINES = 4
SOURCES = 64
PAIR = 2
TOKENS = SOURCES * PAIR
ROWS = HD // SOURCES
COLS = D // (CORES * LINES)
HALF = D // CORES
SPLIT = (ROWS + 1) // 2
F32 = jnp.float32
BF16 = jnp.bfloat16

AXES = {"line": LINES, "core": CORES, "x": 4, "y": 2, "z": 8}
OTHERS = ("x", "y", "z")
W_LANES = ROWS * HALF // PAIR

AT_U = 0
AT_Q = AT_U + D
AT_K = AT_Q + HD
AT_V = AT_K + HD
IN_LANES = AT_V + HD
AT_G = 4 * HD
OUT_LANES = AT_G + SPLIT * COLS


def iota(shape, dim):
    return lax.broadcasted_iota(jnp.int32, shape, dim)


def order_matrix():
    feature, place = iota((HD, HD), 0), iota((HD, HD), 1)
    return (feature == ROWS * (place & (SOURCES - 1)) + (place >> 6)).astype(BF16)


def head_mask(head):
    return (((iota((1, HD), 1) & (SOURCES - 1)) >> 3) == head).astype(BF16)


def dot(a, b, dims, kind=F32):
    return lax.dot_general(a, b, (dims, ((), ())), preferred_element_type=F32).astype(kind)


NN = ((1,), (0,))
NT = ((1,), (1,))
TN = ((0,), (0,))


def spread(x):
    return x.reshape(SOURCES, PAIR, x.shape[-1])


def repeat_kernel(line_ref, w0, w1, w2, w3, x_ref, slots):
    for s, ref in enumerate((w0, w1, w2, w3)):
        slots[s, :ROWS, :] = ref[...].astype(F32)
    line = line_ref[0]
    blocks = [slots[lax.rem(line - b + LINES, LINES)] for b in range(LINES)]
    full = jnp.concatenate(blocks, axis=1)
    rows = [full[i : i + 1] for i in range(ROWS)]
    mid = ROWS // 2
    top = jnp.concatenate(rows[:mid] + [rows[mid][:, : HALF // 2]], axis=1)
    low = jnp.concatenate([rows[mid][:, HALF // 2 :]] + rows[mid + 1 :], axis=1)
    odd = (iota((TOKENS, W_LANES), 0) & 1) == 1
    x_ref[...] = spread(jnp.where(odd, low, top).astype(BF16))


def pack_kernel(core_ref, q_ref, k_ref, v_ref, u_ref, x_ref, feats, up, packed, sems):
    copies = []
    for h in range(4):
        part = pl.ds(h * (TOKENS // 4), TOKENS // 4)
        copies.append(pltpu.make_async_copy(u_ref.at[part], up.at[part], sems.at[h]))
    for n, ref in enumerate((q_ref, k_ref, v_ref)):
        for h in range(2):
            part = pl.ds(h * (HD // 2), HD // 2)
            copies.append(
                pltpu.make_async_copy(ref.at[part], feats.at[n, part], sems.at[4 + 2 * n + h])
            )
    for copy in copies:
        copy.start()

    def out(n, at, lanes):
        part = pl.ds(at, lanes)
        return pltpu.make_async_copy(
            packed.at[:, :, part], x_ref.at[:, :, part], sems.at[10 + n]
        )

    outs = [out(0, AT_U, D), out(1, AT_Q, 2 * HD), out(2, AT_V, HD)]
    order = order_matrix()
    for copy in copies[:4]:
        copy.wait()
    first = core_ref[0] == 0
    mine, theirs = [], []
    for line in range(LINES):
        a = up[:, (2 * line) * COLS : (2 * line + 1) * COLS]
        b = up[:, (2 * line + 1) * COLS : (2 * line + 2) * COLS]
        mine.append(jnp.where(first, a, b))
        theirs.append(jnp.where(first, b, a))
    packed[:, :, AT_U : AT_U + D] = spread(jnp.concatenate(mine + theirs, axis=1))
    outs[0].start()
    for n, at in enumerate((AT_Q, AT_K, AT_V)):
        copies[4 + 2 * n].wait()
        copies[5 + 2 * n].wait()
        packed[:, :, at : at + HD] = spread(dot(feats[n], order, TN, BF16))
        if n > 0:
            outs[n].start()
    for copy in outs:
        copy.wait()


def weight_kernel(raw_ref, w_ref):
    pick = iota((SOURCES, TOKENS), 1) - PAIR * iota((SOURCES, TOKENS), 0)
    raw = raw_ref[...].reshape(TOKENS, W_LANES)
    top = dot((pick == 0).astype(BF16), raw, NN, BF16)
    low = dot((pick == 1).astype(BF16), raw, NN, BF16)
    mid, part = ROWS // 2, HALF // 2
    for i in range(ROWS):
        at = slice(i * SOURCES, (i + 1) * SOURCES)
        if i < mid:
            w_ref[at, :] = top[:, i * HALF : (i + 1) * HALF]
        elif i == mid:
            w_ref[at, :part] = top[:, i * HALF :]
            w_ref[at, part:] = low[:, :part]
        else:
            w_ref[at, :] = low[:, part + (i - mid - 1) * HALF : part + (i - mid) * HALF]


def rows_of(x_ref, at, lanes):
    return x_ref[:, :, at : at + lanes].reshape(TOKENS, lanes)


def scale_upstream(x_ref, gate_ref):
    return (gate_ref[...] * rows_of(x_ref, AT_U, D).astype(F32)).astype(BF16)


def forward_kernel(gate_ref, x_ref, probs_ref, swap_ref, mine_ref):
    q, k, v = (rows_of(x_ref, at, HD) for at in (AT_Q, AT_K, AT_V))
    factor = 1.0 / jnp.sqrt(F32(HEAD))
    same = ((iota((TOKENS, TOKENS), 0) ^ iota((TOKENS, TOKENS), 1)) & 1) == 0
    low, v_rows = [], []
    for h in range(HEADS):
        mask = head_mask(h)
        scores = dot(q * mask, k, NT) * factor
        scores = jnp.where(same, scores, -jnp.inf)
        expd = jnp.exp(scores - jnp.max(scores, axis=-1, keepdims=True))
        probs = expd / jnp.sum(expd, axis=-1, keepdims=True)
        probs_ref[h] = probs
        low.append(probs.astype(BF16))
        v_rows.append(v * mask)
    attended = dot(jnp.concatenate(low, axis=1), jnp.concatenate(v_rows, axis=0), NN, BF16)
    scaled = scale_upstream(x_ref, gate_ref)
    swap_ref[:, :HD] = attended
    swap_ref[:, HD:] = scaled[:, HALF:]
    mine_ref[...] = scaled[:, :HALF]


def share_kernel(line_ref, swap_ref, got_ref, mine_ref, o0_ref, o1_ref, o2_ref, o3_ref, packed):
    share = dot(swap_ref[:, :HD], mine_ref[...], TN) + dot(got_ref[:, :HD], got_ref[:, HD:], TN)
    share = share.astype(BF16)
    for b in range(LINES):
        for i in range(ROWS):
            packed[b, :, i * COLS : (i + 1) * COLS] = share[
                i * SOURCES : (i + 1) * SOURCES, b * COLS : (b + 1) * COLS
            ]
    line = line_ref[0]
    for s, ref in enumerate((o0_ref, o1_ref, o2_ref, o3_ref)):
        ref[...] = packed[lax.rem(line + s, LINES)]


def backward_kernel(gate_ref, x_ref, probs_ref, wm_ref, wt_ref, swap_ref, sum_ref, z_ref):
    z_ref[:, :, :HD] = spread(swap_ref[:, :HD])
    z_ref[:, :, AT_G:OUT_LANES] = spread(sum_ref[...])
    q, k, v = (rows_of(x_ref, at, HD) for at in (AT_Q, AT_K, AT_V))
    factor = 1.0 / jnp.sqrt(F32(HEAD))
    scaled = scale_upstream(x_ref, gate_ref)
    grad = dot(scaled[:, :HALF], wm_ref[...], NT) + dot(scaled[:, HALF:], wt_ref[...], NT)
    grad = grad.astype(BF16)
    low, score_grads, g_rows, q_rows, k_rows = [], [], [], [], []
    for h in range(HEADS):
        mask = head_mask(h)
        g_head = grad * mask
        probs = probs_ref[h]
        prob_grad = dot(g_head, v, NT)
        inner = jnp.sum(probs * prob_grad, axis=-1, keepdims=True)
        score_grads.append((probs * (prob_grad - inner)).astype(BF16))
        low.append(probs.astype(BF16))
        g_rows.append(g_head)
        q_rows.append(q * mask)
        k_rows.append(k * mask)
    wide = jnp.concatenate(score_grads, axis=1)
    tall = jnp.concatenate(score_grads, axis=0)
    dq = (dot(wide, jnp.concatenate(k_rows, axis=0), NN) * factor).astype(BF16)
    dk = (dot(tall, jnp.concatenate(q_rows, axis=0), TN) * factor).astype(BF16)
    dv = dot(jnp.concatenate(low, axis=0), jnp.concatenate(g_rows, axis=0), TN, BF16)
    for n, x in enumerate((dq, dk, dv)):
        z_ref[:, :, (n + 1) * HD : (n + 2) * HD] = spread(x)


def sum_kernel(p0_ref, p1_ref, p2_ref, p3_ref, o_ref):
    total = sum(ref[...].astype(F32) for ref in (p0_ref, p1_ref, p2_ref, p3_ref)).astype(BF16)
    lanes = SPLIT * COLS
    pad = jnp.zeros((SOURCES, PAIR * lanes - ROWS * COLS), BF16)
    low = jnp.concatenate([total[:, lanes:], pad], axis=1)
    put = iota((TOKENS, SOURCES), 0) - PAIR * iota((TOKENS, SOURCES), 1)
    mixed = dot((put == 0).astype(BF16), total[:, :lanes], NN) + dot((put == 1).astype(BF16), low, NN)
    o_ref[...] = mixed.astype(BF16)


def final_kernel(
    core_ref, gate_ref, z_ref, wm_ref, wt_ref, out_ref, dq_ref, dk_ref, dv_ref, wg_ref
):
    att = rows_of(z_ref, 0, HD)
    gate = gate_ref[...]
    mine = (gate[:, :HALF] * dot(att, wm_ref[...], NN)).astype(BF16)
    theirs = (gate[:, HALF:] * dot(att, wt_ref[...], NN)).astype(BF16)
    first = core_ref[0] == 0
    parts = []
    for line in range(LINES):
        a = mine[:, line * COLS : (line + 1) * COLS]
        b = theirs[:, line * COLS : (line + 1) * COLS]
        parts += [jnp.where(first, a, b), jnp.where(first, b, a)]
    out_ref[...] = jnp.concatenate(parts, axis=1)
    order = order_matrix()
    for n, ref in enumerate((dq_ref, dk_ref, dv_ref)):
        ref[...] = dot(order, rows_of(z_ref, (n + 1) * HD, HD), NT, BF16)
    pick = ((iota((8, TOKENS), 1) & 1) == iota((8, TOKENS), 0)).astype(BF16)
    sums = dot(pick, rows_of(z_ref, AT_G, SPLIT * COLS), NN)
    for i in range(ROWS):
        j, lane = i // SPLIT, (i % SPLIT) * COLS
        wg_ref[i : i + 1, :] = sums[j : j + 1, lane : lane + COLS]


def call(kernel, outs, args, scalars=0, far=0, far_out=False, scratch=(), flops=10**8, limit=24):
    smem = [pl.BlockSpec(memory_space=pltpu.SMEM)] * scalars
    vmem = [pl.BlockSpec(memory_space=pltpu.VMEM)] * (len(args) - scalars - far)
    hbm = [pl.BlockSpec(memory_space=pltpu.HBM)] * far
    moved = sum(int(np.prod(x.shape)) * x.dtype.itemsize for x in [*args, *outs])
    single = len(outs) == 1
    out_spec = [pl.BlockSpec(memory_space=pltpu.HBM if far_out else pltpu.VMEM)] * len(outs)
    return pl.pallas_call(
        kernel,
        out_shape=outs[0] if single else outs,
        in_specs=smem + vmem + hbm,
        out_specs=out_spec[0] if single else out_spec,
        scratch_shapes=scratch,
        cost_estimate=pl.CostEstimate(flops=flops, bytes_accessed=moved, transcendentals=0),
        compiler_params=pltpu.CompilerParams(vmem_limit_bytes=limit * 1024 * 1024),
    )(*args)


def shape(*dims, kind=BF16):
    return jax.ShapeDtypeStruct(dims, kind)


def column_order():
    cols = np.arange(D).reshape(LINES, CORES, COLS)
    return [np.concatenate([cols[:, c].ravel(), cols[:, 1 - c].ravel()]) for c in range(CORES)]


def shards(queries, keys, values, out_weight, upstream, timestep):
    core = lax.axis_index("core").astype(jnp.int32)
    core_s, line_s = core.reshape(1), lax.axis_index("line").astype(jnp.int32).reshape(1)

    def shift_line(x, s):
        return lax.ppermute(x, "line", [(d, (d + s) % LINES) for d in range(LINES)])

    def swap_core(x):
        return lax.ppermute(x, "core", [(0, 1), (1, 0)])

    orders = [o.astype(np.float32) for o in column_order()]
    index = jnp.where(core == 0, orders[0], orders[1])
    freq = jnp.exp(-jnp.log(10000.0) * index / D)
    gate = (1.5 + jnp.sin(timestep.astype(F32)[0] * freq)).reshape(1, D)

    flat = [x.reshape(TOKENS, HD).T for x in (queries, keys, values)]
    sent = call(
        pack_kernel,
        [shape(SOURCES, PAIR, IN_LANES)],
        (core_s, *flat, upstream.reshape(TOKENS, D)),
        scalars=1,
        far=4,
        far_out=True,
        limit=60,
        scratch=[
            pltpu.VMEM((3, HD, TOKENS), BF16),
            pltpu.VMEM((TOKENS, D), BF16),
            pltpu.VMEM((SOURCES, PAIR, IN_LANES), BF16),
            pltpu.SemaphoreType.DMA((13,)),
        ],
    )
    own_w, _ = lax.optimization_barrier((out_weight, sent))
    weights = [own_w] + [shift_line(own_w, s) for s in range(1, LINES)]
    slab = lax.all_to_all(sent, OTHERS, split_axis=0, concat_axis=0, tiled=True)
    w_sent = call(
        repeat_kernel,
        [shape(SOURCES, PAIR, W_LANES)],
        (line_s, *weights),
        scalars=1,
        scratch=[pltpu.VMEM((LINES, 16, COLS), F32)],
    )
    w_sent, _ = lax.optimization_barrier((w_sent, slab))
    w_raw = lax.all_to_all(w_sent, OTHERS, split_axis=0, concat_axis=0, tiled=True)

    probs, swap, mine = call(
        forward_kernel,
        [shape(HEADS, TOKENS, TOKENS, kind=F32), shape(TOKENS, HD + HALF), shape(TOKENS, HALF)],
        (gate, slab),
    )
    got = swap_core(swap)
    pieces = call(
        share_kernel,
        [shape(SOURCES, ROWS * COLS)] * LINES,
        (line_s, swap, got, mine),
        scalars=1,
        scratch=[pltpu.VMEM((LINES, SOURCES, ROWS * COLS), BF16)],
    )
    sums = [pieces[0]] + [shift_line(pieces[s], s) for s in range(1, LINES)]
    w_raw, _ = lax.optimization_barrier((w_raw, pieces[0]))
    w_mine = call(weight_kernel, [shape(HD, HALF)], (w_raw,))
    w_theirs = swap_core(w_mine)
    total = call(sum_kernel, [shape(TOKENS, SPLIT * COLS)], sums, flops=10**10)
    back = call(
        backward_kernel,
        [shape(SOURCES, PAIR, OUT_LANES)],
        (gate, slab, probs, w_mine, w_theirs, swap, total),
        flops=10**9,
    )
    frame = lax.all_to_all(back, OTHERS, split_axis=0, concat_axis=0, tiled=True)
    output, dq, dk, dv, weight_grad = call(
        final_kernel,
        [shape(TOKENS, D)] + [shape(HD, TOKENS)] * 3 + [shape(ROWS, COLS, kind=F32)],
        (core_s, gate, frame, w_mine, w_theirs),
        scalars=1,
    )
    dims = queries.shape
    return (output.reshape(upstream.shape), *(x.T.reshape(dims) for x in (dq, dk, dv)), weight_grad)


def solution(mesh):
    cut = jax.sharding.Mesh(mesh.devices.reshape(tuple(AXES.values())), tuple(AXES))
    dp, tm = ("line", "core"), OTHERS
    act = P(dp, tm, None, None)
    return jax.shard_map(
        shards,
        mesh=cut,
        in_specs=(act, act, act, P(tm, dp), act, P(dp)),
        out_specs=(act, act, act, act, P(tm, dp)),
        check_vma=False,
    )
```
